128 devices in a mesh: row: 8 (over z_hi, x), col: 16 (over z_lo, y, core).
Axes of the slice: x: 4, y: 4, z: 4 (z_hi: 2, z_lo: 2; z = z_hi * 2 + z_lo), core: 2. Of those that a mesh axis runs over, the one named last changes fastest.
Arguments:
- pair_state: bfloat16 [512, 512, 128], P('row', 'col'), may hold values from -6 to 6
- proj_weight: bfloat16 [2, 128, 640], replicated, may hold values from -0.5 to 0.5
- out_weight: bfloat16 [2, 128, 128], replicated, may hold values from -0.5 to 0.5
Outputs:
- pair_out: bfloat16 [512, 512, 128], P('row', 'col')
The draws below stay inside these ranges and needn't reach their ends.
All inputs are finite; a program needn't handle non-finite values.
Results may differ from the reference program's by a relative error of at most 0.015.
Values may be sent and summed in bfloat16 or wider, within the bound.
A program may use at most 128 MiB of HBM per device.

```python
import jax
import jax.numpy as jnp
from jax import lax

CZ = 128
CH = 128
N = 512


def levels(key, extent, split, smallest, top_value):
    loudness = 1.0
    for position, parts in split:
        draws = jax.random.uniform(jax.random.fold_in(jax.random.fold_in(key, 6), position), (parts,), jnp.float32, smallest / len(split), top_value / len(split))
        loudness = loudness * jnp.repeat(jnp.exp(draws), extent[position] // parts).reshape((-1,) + (1,) * (len(extent) - 1 - position))
    return loudness


def scatter_about(rng, shape, scale, bound, shards=(), dtype=jnp.bfloat16):
    gain = levels(rng, shape, shards, -0.22, 0.18) if shards else 1.0
    array = jax.random.normal(rng, shape, jnp.float32) * scale * gain
    return jnp.minimum(jnp.maximum(array, -bound), bound).astype(dtype)


def setup_inputs(seed: int = 0) -> dict:
    key_list = jax.random.split(jax.random.key(seed), 4)
    return {
        "pair_state": scatter_about(key_list[0], (N, N, CZ), 1.0, 6.0, ((0, 8), (1, 16))),
        "proj_weight": scatter_about(key_list[1], (2, CZ, 4 * CH + CZ), CZ ** -0.5, 0.5),
        "out_weight": scatter_about(key_list[2], (2, CH, CZ), CH ** -0.5, 0.5),
    }


def normalize(values):
    center = values - lax.optimization_barrier(jnp.mean(values, axis=-1, keepdims=True))
    spread = lax.optimization_barrier(jnp.mean(center * center, axis=-1, keepdims=True))
    return center * jax.lax.rsqrt(spread + 1e-05)

def update(pair, weight, out_proj, incoming):
    width = pair.shape[2]
    hidden = out_proj.shape[0]
    normed = normalize(pair.astype(jnp.float32)).astype(jnp.bfloat16)
    projected = jnp.dot(normed.reshape(-1, width), weight, preferred_element_type=jnp.float32)
    left_proj = (jax.nn.sigmoid(projected[:, :hidden]) * projected[:, hidden:2 * hidden]).astype(jnp.bfloat16)
    right_proj = (jax.nn.sigmoid(projected[:, 2 * hidden:3 * hidden]) * projected[:, 3 * hidden:4 * hidden]).astype(jnp.bfloat16)
    gating = jax.nn.sigmoid(projected[:, 4 * hidden:])
    left_proj = left_proj.reshape(N, N, hidden).astype(jnp.float32)
    right_proj = right_proj.reshape(N, N, hidden).astype(jnp.float32)
    if incoming:
        mixed_sum = jnp.einsum('kic,kjc->ijc', left_proj, right_proj)
    else:
        mixed_sum = jnp.einsum('ikc,jkc->ijc', left_proj, right_proj)
    mixnorm = normalize(mixed_sum).astype(jnp.bfloat16).reshape(-1, hidden)
    output = jnp.dot(mixnorm, out_proj, preferred_element_type=jnp.float32)
    updated = pair.astype(jnp.float32).reshape(-1, width) + gating * output
    return updated.astype(jnp.bfloat16).reshape(N, N, width)

def reference(pair_state, proj_weight, out_weight):
    first = update(pair_state, proj_weight[0], out_weight[0], False)
    return update(first, proj_weight[1], out_weight[1], True)
```

```python
import functools

import jax
import jax.numpy as jnp
from jax import lax
from jax.experimental import pallas as pl
from jax.experimental.pallas import tpu as pltpu
from jax.sharding import PartitionSpec as P

F32 = jnp.float32
BF16 = jnp.bfloat16
MESH = pl.DeviceIdType.MESH


def sigmoid(x):
    return 0.5 * jnp.tanh(0.5 * x) + 0.5


def normalize(x):
    center = x - jnp.mean(x, axis=0, keepdims=True)
    spread = jnp.mean(center * center, axis=0, keepdims=True)
    return center * lax.rsqrt(spread + 1e-05)


def interleave(even, odd):
    first = jnp.concatenate([even[..., :64], odd[..., :64]], axis=-1)
    second = jnp.concatenate([even[..., 64:], odd[..., 64:]], axis=-1)
    return first, second


def kernel(
    pair_ref,
    proj_ref,
    out_proj_ref,
    out_ref,
    proj_t,
    out_proj_t,
    state,
    normed,
    gating,
    staged,
    mixnorm,
    final,
    left_op0,
    left_op1,
    partial,
    send_left,
    send_right,
    recv_left,
    recv_right,
    sibling_left,
    half_send,
    half_recv,
    send_mixed,
    recv_mixed,
    left_send_sem,
    left_recv_sem,
    right_send_sem,
    right_recv_sem,
    sib_send_sem,
    sib_recv_sem,
    half_send_sem,
    half_recv_sem,
    mixed_send_sem,
    mixed_recv_sem,
):
    r = lax.axis_index("row")
    col = lax.axis_index("col")
    q = col // 2
    core = col % 2
    chip = r * 8 + q

    def device(dest_r, dest_q):
        return (dest_r, dest_q * 2 + core)

    sibling = (r, q * 2 + 1 - core)

    barrier = pltpu.get_barrier_semaphore()

    def greet(d, carry):
        other = lax.rem(chip + d, 64)
        pl.semaphore_signal(barrier, inc=1, device_id=device(other // 8, other % 8), device_id_type=MESH)
        return carry

    lax.fori_loop(1, 64, greet, 0)
    pl.semaphore_signal(barrier, inc=1, device_id=sibling, device_id_type=MESH)

    for u in range(2):
        proj_t[u] = proj_ref[u].T
        out_proj_t[u] = out_proj_ref[u].T

    pair = jnp.swapaxes(pair_ref[...], 0, 1)
    final[...] = pair.reshape(2, 16, 64, 128)

    def load(t, carry):
        for h in range(2):
            block = final[:, 2 * t + h].reshape(128, 128).astype(F32).T
            state[t, :, 128 * h : 128 * h + 128] = block
        normed[t] = normalize(state[t]).astype(BF16)
        return carry

    lax.fori_loop(0, 8, load, 0)

    def gated(u, first, dest):
        def step(t, carry):
            p = jnp.dot(proj_t[u, first : first + 256], normed[t], preferred_element_type=F32)
            value = (sigmoid(p[:128]) * p[128:]).astype(BF16)
            for h in range(2):
                staged[2 * t + h] = value[:, 128 * h : 128 * h + 128]
            return carry

        lax.fori_loop(0, 8, step, 0)
        dest[u] = jnp.swapaxes(staged[...], 0, 1).reshape(64, 2, 16, 128)

    def gate(u):
        def step(t, carry):
            p = jnp.dot(proj_t[u, 512:640], normed[t], preferred_element_type=F32)
            gating[t] = sigmoid(p)
            return carry

        lax.fori_loop(0, 8, step, 0)

    def push(src, dst, send_sem, recv_sem, dest_r, dest_q):
        own = jnp.logical_and(dest_r == r, dest_q == q)

        @pl.when(own)
        def _():
            pltpu.make_async_copy(src, dst, recv_sem).start()

        @pl.when(jnp.logical_not(own))
        def _():
            pltpu.make_async_remote_copy(
                src_ref=src,
                dst_ref=dst,
                send_sem=send_sem,
                recv_sem=recv_sem,
                device_id=device(dest_r, dest_q),
                device_id_type=MESH,
            ).start()

    def send_all_left(u):
        slot = recv_left.at[0, r, q] if u == 0 else recv_left.at[1, q, r]

        def step(d, carry):
            other = lax.rem(chip + 37 * d, 64)
            push(send_left.at[u, other], slot, left_send_sem.at[u], left_recv_sem.at[u], other // 8, other % 8)
            return carry

        lax.fori_loop(0, 64, step, 0)

    def send_all_right(u):
        slot = recv_right.at[0, r, q] if u == 0 else recv_right.at[1, q, r]
        mine = r // 2 if u == 0 else q // 2

        def step(d, carry):
            group = lax.rem(mine + 4 - d // 16, 4)
            one, eight = (d // 8) % 2, d % 8
            if u == 0:
                dest_r, dest_q = group * 2 + (one + r) % 2, (eight + q) % 8
            else:
                dest_r, dest_q = (eight + r) % 8, group * 2 + (one + q) % 2
            push(
                send_right.at[u, dest_r * 8 + dest_q],
                slot,
                right_send_sem.at[u],
                right_recv_sem.at[u, mine],
                dest_r,
                dest_q,
            )
            return carry

        lax.fori_loop(0, 64, step, 0)

    def give_back(u, group, c, value):
        for qq in range(2):
            for m in range(4):
                lower = value[qq, :16, 128 * m : 128 * m + 128]
                upper = value[qq, 16:, 128 * m : 128 * m + 128]
                first, second = interleave(lower, upper)
                send_mixed[u, 2 * group + qq, 2 * m, c] = first
                send_mixed[u, 2 * group + qq, 2 * m + 1, c] = second

    def send_back(u, group):
        def step(d, carry):
            dest_q, dest_r = 2 * group + d // 8, (r + d) % 8
            push(
                send_mixed.at[u, dest_q, dest_r],
                recv_mixed.at[u, chip],
                mixed_send_sem.at[u],
                mixed_recv_sem.at[u],
                dest_r,
                dest_q,
            )
            return carry

        lax.fori_loop(0, 16, step, 0)

    def wait_all(ref, sem):
        pltpu.make_async_copy(ref, ref, sem).wait()

    def outgoing():
        wait_all(recv_left.at[0], left_recv_sem.at[0])
        for c in range(2):
            for m in range(4):
                first, second = interleave(recv_left[0, 2 * m, :, c], recv_left[0, 2 * m + 1, :, c])
                left_op0[c, 0, :, :, 128 * m : 128 * m + 128] = first
                left_op0[c, 1, :, :, 128 * m : 128 * m + 128] = second

        def half_copy(t):
            return pltpu.make_async_remote_copy(
                src_ref=half_send.at[t],
                dst_ref=half_recv.at[t],
                send_sem=half_send_sem.at[t],
                recv_sem=half_recv_sem.at[t],
                device_id=sibling,
                device_id_type=MESH,
            )

        def finish_group(t):
            group = lax.rem(r // 2 + t, 4)
            half_copy(t).wait_recv()
            for c in range(2):
                total = partial[t % 2, c, :, core] + half_recv[t, c].astype(F32)
                give_back(0, group, c, total.astype(BF16))
            send_back(0, group)

        for t in range(4):
            group = lax.rem(r // 2 + t, 4)
            wait_all(recv_right.at[0, pl.ds(2 * group, 2)], right_recv_sem.at[0, group])
            for c in range(2):
                first, second = interleave(recv_right[0, 2 * group, :, c], recv_right[0, 2 * group + 1, :, c])
                right = jnp.concatenate([first.reshape(128, 128), second.reshape(128, 128)], axis=0)
                product = lax.dot_general(
                    right, left_op0[c].reshape(256, 512), (((0,), (0,)), ((), ())), preferred_element_type=F32
                )
                partial[t % 2, c] = product.reshape(2, 2, 32, 512)
                half_send[t, c] = partial[t % 2, c, :, 1 - core].astype(BF16)
            half_copy(t).start()
            if t:
                finish_group(t - 1)
        finish_group(3)
        for t in range(4):
            half_copy(t).wait_send()

    def incoming():
        wait_all(recv_left.at[1], left_recv_sem.at[1])
        swap = pltpu.make_async_remote_copy(
            src_ref=recv_left.at[1],
            dst_ref=sibling_left,
            send_sem=sib_send_sem,
            recv_sem=sib_recv_sem,
            device_id=sibling,
            device_id_type=MESH,
        )
        swap.start()

        def arrange(blocks, which):
            for c in range(2):
                for m in range(4):
                    first, second = interleave(blocks[:, 2 * m, c], blocks[:, 2 * m + 1, c])
                    left_op1[c, :, which, 0, :, 128 * m : 128 * m + 128] = first
                    left_op1[c, :, which, 1, :, 128 * m : 128 * m + 128] = second

        arrange(recv_left.at[1], core)
        swap.wait_recv()
        arrange(sibling_left, 1 - core)

        for t in range(4):
            group = lax.rem(q // 2 + t, 4)
            wait_all(recv_right.at[1, pl.ds(2 * group, 2)], right_recv_sem.at[1, group])
            for c in range(2):
                columns = []
                for m in range(4):
                    even = recv_right[1, pl.ds(2 * group, 2), 2 * m, c]
                    odd = recv_right[1, pl.ds(2 * group, 2), 2 * m + 1, c]
                    columns.append(jnp.stack(interleave(even, odd), axis=1).reshape(64, 128))
                right = jnp.concatenate(columns, axis=1)
                product = lax.dot_general(
                    right, left_op1[c].reshape(512, 512), (((1,), (1,)), ((), ())), preferred_element_type=F32
                )
                give_back(1, group, c, product.astype(BF16).reshape(2, 32, 512))
            send_back(1, group)
        swap.wait_send()

    def absorb(u):
        wait_all(recv_mixed.at[u], mixed_recv_sem.at[u])
        mixed = recv_mixed[u].reshape(128, 16, 128).astype(F32)
        norm = jnp.swapaxes(normalize(mixed).astype(BF16), 0, 1)
        for t in range(8):
            for h in range(2):
                mixnorm[t, :, 128 * h : 128 * h + 128] = norm[2 * t + h]

        def step(t, carry):
            output = jnp.dot(out_proj_t[u], mixnorm[t], preferred_element_type=F32)
            updated = state[t] + gating[t] * output
            if u == 0:
                updated = updated.astype(BF16).astype(F32)
                state[t] = updated
                normed[t] = normalize(updated).astype(BF16)
            else:
                for h in range(2):
                    block = updated[:, 128 * h : 128 * h + 128].T.astype(BF16)
                    final[:, 2 * t + h] = block.reshape(2, 64, 128)
            return carry

        lax.fori_loop(0, 8, step, 0)

    gated(0, 0, send_left)
    pl.semaphore_wait(barrier, 64)
    send_all_left(0)
    gated(0, 256, send_right)
    send_all_right(0)
    gate(0)
    outgoing()
    absorb(0)
    gated(1, 0, send_left)
    send_all_left(1)
    gated(1, 256, send_right)
    send_all_right(1)
    gate(1)
    incoming()
    absorb(1)
    out_ref[...] = final[...].reshape(32, 64, 128)

    for u in range(2):
        sent = pl.ds(0, 63)
        wait_all(send_left.at[u, sent], left_send_sem.at[u])
        wait_all(send_right.at[u, sent], right_send_sem.at[u])
        wait_all(recv_mixed.at[u, sent], mixed_send_sem.at[u])


def shards(pair_state, proj_weight, out_weight):
    vmem = pl.BlockSpec(memory_space=pltpu.VMEM)
    dma = pltpu.SemaphoreType.DMA
    out = pl.pallas_call(
        kernel,
        out_shape=jax.ShapeDtypeStruct((32, 64, 128), BF16),
        in_specs=[vmem] * 3,
        out_specs=vmem,
        scratch_shapes=[
            pltpu.VMEM((2, 640, 128), BF16),
            pltpu.VMEM((2, 128, 128), BF16),
            pltpu.VMEM((8, 128, 256), F32),
            pltpu.VMEM((8, 128, 256), BF16),
            pltpu.VMEM((8, 128, 256), F32),
            pltpu.VMEM((16, 128, 128), BF16),
            pltpu.VMEM((8, 128, 256), BF16),
            pltpu.VMEM((2, 16, 64, 128), BF16),
            pltpu.VMEM((2, 2, 8, 16, 512), BF16),
            pltpu.VMEM((2, 8, 2, 2, 16, 512), BF16),
            pltpu.VMEM((2, 2, 2, 2, 32, 512), F32),
            pltpu.VMEM((2, 64, 2, 16, 128), BF16),
            pltpu.VMEM((2, 64, 2, 16, 128), BF16),
            pltpu.VMEM((2, 8, 8, 2, 16, 128), BF16),
            pltpu.VMEM((2, 8, 8, 2, 16, 128), BF16),
            pltpu.VMEM((8, 8, 2, 16, 128), BF16),
            pltpu.VMEM((4, 2, 2, 32, 512), BF16),
            pltpu.VMEM((4, 2, 2, 32, 512), BF16),
            pltpu.VMEM((2, 8, 8, 2, 16, 128), BF16),
            pltpu.VMEM((2, 64, 2, 16, 128), BF16),
            dma((2,)),
            dma((2,)),
            dma((2,)),
            dma((2, 4)),
            dma,
            dma,
            dma((4,)),
            dma((4,)),
            dma((2,)),
            dma((2,)),
        ],
        compiler_params=pltpu.CompilerParams(
            collective_id=0, has_side_effects=True, vmem_limit_bytes=48 * 2**20
        ),
    )(pair_state, proj_weight, out_weight)
    return jnp.transpose(out, (1, 0, 2))


def solution(mesh):
    in_specs = (P("row", "col", None), P(), P())
    out_specs = P("row", "col", None)
    return jax.shard_map(shards, mesh=mesh, in_specs=in_specs, out_specs=out_specs, check_vma=False)
```

```python
import functools

import jax
import jax.numpy as jnp
from jax import lax
from jax.experimental import pallas as pl
from jax.experimental.pallas import tpu as pltpu
from jax.sharding import PartitionSpec as P

F32 = jnp.float32
BF16 = jnp.bfloat16
MESH = pl.DeviceIdType.MESH


def sigmoid(x):
    return 0.5 * jnp.tanh(0.5 * x) + 0.5


def normalize(x):
    center = x - jnp.mean(x, axis=0, keepdims=True)
    spread = jnp.mean(center * center, axis=0, keepdims=True)
    return center * lax.rsqrt(spread + 1e-05)


def interleave(even, odd):
    first = jnp.concatenate([even[..., :64], odd[..., :64]], axis=-1)
    second = jnp.concatenate([even[..., 64:], odd[..., 64:]], axis=-1)
    return first, second


def kernel(
    pair_hbm,
    proj_hbm,
    out_proj_hbm,
    out_ref,
    pair_ref,
    proj_ref,
    out_proj_ref,
    proj_t,
    out_proj_t,
    state,
    normed,
    gating,
    staged,
    mixnorm,
    final,
    left_op0,
    left_op1,
    partial,
    send_left,
    send_right,
    recv_left,
    recv_right,
    sibling_left,
    half_send,
    half_recv,
    send_mixed,
    recv_mixed,
    left_send_sem,
    left_recv_sem,
    right_send_sem,
    right_recv_sem,
    sib_send_sem,
    sib_recv_sem,
    half_send_sem,
    half_recv_sem,
    mixed_send_sem,
    mixed_recv_sem,
    load_sem,
):
    r = lax.axis_index("row")
    col = lax.axis_index("col")
    q = col // 2
    core = col % 2
    chip = r * 8 + q

    def around(place):
        return [lax.rem(place // 4 + d // 4, 2) * 4 + lax.rem(place % 4 + d % 4, 4) for d in range(8)]

    rs, qs = around(r), around(q)
    cols = [dest_q * 2 + core for dest_q in qs]
    sibling = (r, q * 2 + 1 - core)
    others = [(d // 8, d % 8) for d in sorted(range(1,64), key=lambda e: (e * 7919) % 1009)]

    loads = [
        pltpu.make_async_copy(src, dst, load_sem.at[i])
        for i, (src, dst) in enumerate(
            ((pair_hbm, pair_ref), (proj_hbm, proj_ref), (out_proj_hbm, out_proj_ref))
        )
    ]
    for load in loads:
        load.start()

    barrier = pltpu.get_barrier_semaphore()

    for dr, dq in others:
        pl.semaphore_signal(barrier, inc=1, device_id=(rs[dr], cols[dq]), device_id_type=MESH)
    pl.semaphore_signal(barrier, inc=1, device_id=sibling, device_id_type=MESH)

    loads[0].wait()
    pair = jnp.swapaxes(pair_ref[...], 0, 1)
    final[...] = pair.reshape(2, 16, 64, 128)

    def enter(t, carry):
        for h in range(2):
            block = final[:, 2 * t + h].reshape(128, 128).astype(F32).T
            state[t, :, 128 * h : 128 * h + 128] = block
        normed[t] = normalize(state[t]).astype(BF16)
        return carry

    lax.fori_loop(0, 8, enter, 0, unroll=8)
    for load in loads[1:]:
        load.wait()
    for u in range(2):
        proj_t[u] = proj_ref[u].T
        out_proj_t[u] = out_proj_ref[u].T

    def gated(u, first, dest):
        def step(t, carry):
            p = jnp.dot(proj_t[u, first : first + 256], normed[t], preferred_element_type=F32)
            value = (sigmoid(p[:128]) * p[128:]).astype(BF16)
            for h in range(2):
                staged[2 * t + h] = value[:, 128 * h : 128 * h + 128]
            return carry

        lax.fori_loop(0, 8, step, 0, unroll=8)
        dest[u] = jnp.swapaxes(staged[...], 0, 1).reshape(8, 8, 2, 16, 128)

    def gate(u):
        def step(t, carry):
            p = jnp.dot(proj_t[u, 512:640], normed[t], preferred_element_type=F32)
            gating[t] = sigmoid(p)
            return carry

        lax.fori_loop(0, 8, step, 0, unroll=8)

    def push(src, dst, send_sem, recv_sem, device):
        pltpu.make_async_remote_copy(
            src_ref=src,
            dst_ref=dst,
            send_sem=send_sem,
            recv_sem=recv_sem,
            device_id=device,
            device_id_type=MESH,
        ).start()

    def send_all_left(u):
        slot = recv_left.at[0, r, q] if u == 0 else recv_left.at[1, q, r]
        pltpu.make_async_copy(send_left.at[u, r, q], slot, left_recv_sem.at[u]).start()
        for dr, dq in others:
            push(
                send_left.at[u, rs[dr], qs[dq]],
                slot,
                left_send_sem.at[u],
                left_recv_sem.at[u],
                (rs[dr], cols[dq]),
            )

    def send_all_right(u):
        slot = recv_right.at[0, r, q] if u == 0 else recv_right.at[1, q, r]
        mine = r // 2 if u == 0 else q // 2
        recv_sem = right_recv_sem.at[u, mine]
        pltpu.make_async_copy(send_right.at[u, r, q], slot, recv_sem).start()
        for t in range(4):
            pair = lax.rem(mine + 4 - t, 4) * 2
            first = r if u == 0 else q
            near = [pair + lax.rem(first + one, 2) for one in range(2)]
            for one in range(2):
                for d in range(8):
                    if t == 0 and one == 0 and d == 0:
                        continue
                    dest_r, dest_q = (near[one], qs[d]) if u == 0 else (rs[d], near[one])
                    push(
                        send_right.at[u, dest_r, dest_q],
                        slot,
                        right_send_sem.at[u],
                        recv_sem,
                        (dest_r, dest_q * 2 + core),
                    )

    def give_back(u, group, c, value):
        for qq in range(2):
            for m in range(4):
                lower = value[qq, :16, 128 * m : 128 * m + 128]
                upper = value[qq, 16:, 128 * m : 128 * m + 128]
                first, second = interleave(lower, upper)
                send_mixed[u, 2 * group + qq, 2 * m, c] = first
                send_mixed[u, 2 * group + qq, 2 * m + 1, c] = second

    def send_back(u, group):
        slot = recv_mixed.at[u, chip]
        for one in range(2):
            dest_q = 2 * group + one
            dest_col = dest_q * 2 + core
            here = dest_q == q

            @pl.when(here)
            def _():
                pltpu.make_async_copy(send_mixed.at[u, dest_q, r], slot, mixed_recv_sem.at[u]).start()

            @pl.when(jnp.logical_not(here))
            def _():
                push(
                    send_mixed.at[u, dest_q, r], slot, mixed_send_sem.at[u], mixed_recv_sem.at[u], (r, dest_col)
                )

            for d in range(1, 8):
                push(
                    send_mixed.at[u, dest_q, rs[d]],
                    slot,
                    mixed_send_sem.at[u],
                    mixed_recv_sem.at[u],
                    (rs[d], dest_col),
                )

    def wait_all(ref, sem):
        pltpu.make_async_copy(ref, ref, sem).wait()

    def outgoing():
        wait_all(recv_left.at[0], left_recv_sem.at[0])
        for c in range(2):
            for m in range(4):
                first, second = interleave(recv_left[0, 2 * m, :, c], recv_left[0, 2 * m + 1, :, c])
                left_op0[c, 0, :, :, 128 * m : 128 * m + 128] = first
                left_op0[c, 1, :, :, 128 * m : 128 * m + 128] = second

        def half_copy(t):
            return pltpu.make_async_remote_copy(
                src_ref=half_send.at[t],
                dst_ref=half_recv.at[t],
                send_sem=half_send_sem.at[t],
                recv_sem=half_recv_sem.at[t],
                device_id=sibling,
                device_id_type=MESH,
            )

        def finish_group(t):
            group = lax.rem(r // 2 + t, 4)
            half_copy(t).wait_recv()
            for c in range(2):
                total = partial[t % 2, c, :, core] + half_recv[t, c].astype(F32)
                give_back(0, group, c, total.astype(BF16))
            send_back(0, group)

        for t in range(4):
            group = lax.rem(r // 2 + t, 4)
            wait_all(recv_right.at[0, pl.ds(2 * group, 2)], right_recv_sem.at[0, group])
            for c in range(2):
                first, second = interleave(recv_right[0, 2 * group, :, c], recv_right[0, 2 * group + 1, :, c])
                right = jnp.concatenate([first.reshape(128, 128), second.reshape(128, 128)], axis=0)
                product = lax.dot_general(
                    right, left_op0[c].reshape(256, 512), (((0,), (0,)), ((), ())), preferred_element_type=F32
                )
                partial[t % 2, c] = product.reshape(2, 2, 32, 512)
                half_send[t, c] = partial[t % 2, c, :, 1 - core].astype(BF16)
            half_copy(t).start()
            if t:
                finish_group(t - 1)
        finish_group(3)
        for t in range(4):
            half_copy(t).wait_send()

    def incoming():
        wait_all(recv_left.at[1], left_recv_sem.at[1])
        swap = pltpu.make_async_remote_copy(
            src_ref=recv_left.at[1],
            dst_ref=sibling_left,
            send_sem=sib_send_sem,
            recv_sem=sib_recv_sem,
            device_id=sibling,
            device_id_type=MESH,
        )
        swap.start()

        def arrange(blocks, which):
            for c in range(2):
                for m in range(4):
                    first, second = interleave(blocks[:, 2 * m, c], blocks[:, 2 * m + 1, c])
                    left_op1[c, :, which, 0, :, 128 * m : 128 * m + 128] = first
                    left_op1[c, :, which, 1, :, 128 * m : 128 * m + 128] = second

        arrange(recv_left.at[1], core)
        swap.wait_recv()
        arrange(sibling_left, 1 - core)

        for t in range(4):
            group = lax.rem(q // 2 + t, 4)
            wait_all(recv_right.at[1, pl.ds(2 * group, 2)], right_recv_sem.at[1, group])
            for c in range(2):
                columns = []
                for m in range(4):
                    even = recv_right[1, pl.ds(2 * group, 2), 2 * m, c]
                    odd = recv_right[1, pl.ds(2 * group, 2), 2 * m + 1, c]
                    columns.append(jnp.stack(interleave(even, odd), axis=1).reshape(64, 128))
                right = jnp.concatenate(columns, axis=1)
                product = lax.dot_general(
                    right, left_op1[c].reshape(512, 512), (((1,), (1,)), ((), ())), preferred_element_type=F32
                )
                give_back(1, group, c, product.astype(BF16).reshape(2, 32, 512))
            send_back(1, group)
        swap.wait_send()

    def absorb(u):
        wait_all(recv_mixed.at[u], mixed_recv_sem.at[u])
        mixed = recv_mixed[u].reshape(128, 16, 128).astype(F32)
        norm = jnp.swapaxes(normalize(mixed).astype(BF16), 0, 1)
        for t in range(8):
            for h in range(2):
                mixnorm[t, :, 128 * h : 128 * h + 128] = norm[2 * t + h]

        def step(t, carry):
            output = jnp.dot(out_proj_t[u], mixnorm[t], preferred_element_type=F32)
            updated = state[t] + gating[t] * output
            if u == 0:
                updated = updated.astype(BF16).astype(F32)
                state[t] = updated
                normed[t] = normalize(updated).astype(BF16)
            else:
                for h in range(2):
                    block = updated[:, 128 * h : 128 * h + 128].T.astype(BF16)
                    final[:, 2 * t + h] = block.reshape(2, 64, 128)
            return carry

        lax.fori_loop(0, 8, step, 0, unroll=8)

    gated(0, 0, send_left)
    pl.semaphore_wait(barrier, 64)
    send_all_left(0)
    gated(0, 256, send_right)
    send_all_right(0)
    gate(0)
    outgoing()
    absorb(0)
    gated(1, 0, send_left)
    send_all_left(1)
    gated(1, 256, send_right)
    send_all_right(1)
    gate(1)
    incoming()
    absorb(1)
    out_ref[...] = final[...].reshape(32, 64, 128)

    for u in range(2):
        sent = recv_mixed.at[u, pl.ds(0, 63)]
        wait_all(sent, left_send_sem.at[u])
        wait_all(sent, right_send_sem.at[u])
        wait_all(sent, mixed_send_sem.at[u])


def shards(pair_state, proj_weight, out_weight):
    vmem = pl.BlockSpec(memory_space=pltpu.VMEM)
    dma = pltpu.SemaphoreType.DMA
    out = pl.pallas_call(
        kernel,
        out_shape=jax.ShapeDtypeStruct((32, 64, 128), BF16),
        in_specs=[pl.BlockSpec(memory_space=pl.ANY)] * 3,
        out_specs=vmem,
        scratch_shapes=[
            pltpu.VMEM((64, 32, 128), BF16),
            pltpu.VMEM((2, 128, 640), BF16),
            pltpu.VMEM((2, 128, 128), BF16),
            pltpu.VMEM((2, 640, 128), BF16),
            pltpu.VMEM((2, 128, 128), BF16),
            pltpu.VMEM((8, 128, 256), F32),
            pltpu.VMEM((8, 128, 256), BF16),
            pltpu.VMEM((8, 128, 256), F32),
            pltpu.VMEM((16, 128, 128), BF16),
            pltpu.VMEM((8, 128, 256), BF16),
            pltpu.VMEM((2, 16, 64, 128), BF16),
            pltpu.VMEM((2, 2, 8, 16, 512), BF16),
            pltpu.VMEM((2, 8, 2, 2, 16, 512), BF16),
            pltpu.VMEM((2, 2, 2, 2, 32, 512), F32),
            pltpu.VMEM((2, 8, 8, 2, 16, 128), BF16),
            pltpu.VMEM((2, 8, 8, 2, 16, 128), BF16),
            pltpu.VMEM((2, 8, 8, 2, 16, 128), BF16),
            pltpu.VMEM((2, 8, 8, 2, 16, 128), BF16),
            pltpu.VMEM((8, 8, 2, 16, 128), BF16),
            pltpu.VMEM((4, 2, 2, 32, 512), BF16),
            pltpu.VMEM((4, 2, 2, 32, 512), BF16),
            pltpu.VMEM((2, 8, 8, 2, 16, 128), BF16),
            pltpu.VMEM((2, 64, 2, 16, 128), BF16),
            dma((2,)),
            dma((2,)),
            dma((2,)),
            dma((2, 4)),
            dma,
            dma,
            dma((4,)),
            dma((4,)),
            dma((2,)),
            dma((2,)),
            dma((3,)),
        ],
        compiler_params=pltpu.CompilerParams(
            collective_id=0, has_side_effects=True, vmem_limit_bytes=56 * 2**20
        ),
    )(pair_state, proj_weight, out_weight)
    return jnp.transpose(out, (1, 0, 2))


def solution(mesh):
    in_specs = (P("row", "col", None), P(), P())
    out_specs = P("row", "col", None)
    return jax.shard_map(shards, mesh=mesh, in_specs=in_specs, out_specs=out_specs, check_vma=False)
```

```python
import functools

import jax
import jax.numpy as jnp
from jax import lax
from jax.experimental import pallas as pl
from jax.experimental.pallas import tpu as pltpu
from jax.sharding import PartitionSpec as P

F32 = jnp.float32
BF16 = jnp.bfloat16
MESH = pl.DeviceIdType.MESH


def sigmoid(x):
    return 0.5 * jnp.tanh(0.5 * x) + 0.5


def normalize(x):
    center = x - jnp.mean(x, axis=0, keepdims=True)
    spread = jnp.mean(center * center, axis=0, keepdims=True)
    return center * lax.rsqrt(spread + 1e-05)


def interleave(even, odd):
    first = jnp.concatenate([even[..., :64], odd[..., :64]], axis=-1)
    second = jnp.concatenate([even[..., 64:], odd[..., 64:]], axis=-1)
    return first, second


def kernel(
    pair_hbm,
    proj_hbm,
    out_proj_hbm,
    out_ref,
    pair_ref,
    proj_ref,
    out_proj_ref,
    proj_t,
    out_proj_t,
    state,
    normed,
    gating,
    staged,
    mixnorm,
    final,
    left_op0,
    left_op1,
    partial,
    send_left,
    send_left1,
    send_right,
    recv_left,
    recv_left1,
    recv_right,
    sibling_left,
    half_send,
    half_recv,
    send_half,
    recv_half,
    send_whole,
    recv_whole,
    left_send_sem,
    left_recv_sem,
    right_send_sem,
    right_recv_sem,
    sib_send_sem,
    sib_recv_sem,
    half_send_sem,
    half_recv_sem,
    mixed_send_sem,
    mixed_recv_sem,
    load_sem,
):
    r = lax.axis_index("row")
    col = lax.axis_index("col")
    q = col // 2
    core = col % 2
    chip = r * 8 + q

    def around(place):
        return [lax.rem(place // 4 + d // 4, 2) * 4 + lax.rem(place % 4 + d % 4, 4) for d in range(8)]

    rs, qs = around(r), around(q)
    cols = [dest_q * 2 + core for dest_q in qs]
    sibling = (r, q * 2 + 1 - core)
    others = [(d // 8, d % 8) for d in sorted(range(1,64), key=lambda e: (e * 7919) % 1009)]

    loads = [
        pltpu.make_async_copy(src, dst, load_sem.at[i])
        for i, (src, dst) in enumerate(
            ((pair_hbm, pair_ref), (proj_hbm, proj_ref), (out_proj_hbm, out_proj_ref))
        )
    ]
    for load in loads:
        load.start()

    barrier = pltpu.get_barrier_semaphore()

    for dr, dq in others:
        pl.semaphore_signal(barrier, inc=1, device_id=(rs[dr], cols[dq]), device_id_type=MESH)
    pl.semaphore_signal(barrier, inc=1, device_id=sibling, device_id_type=MESH)

    loads[0].wait()
    pair = jnp.swapaxes(pair_ref[...], 0, 1)
    final[...] = pair.reshape(2, 16, 64, 128)

    def enter(t, carry):
        for h in range(2):
            block = final[:, 2 * t + h].reshape(128, 128).astype(F32).T
            state[t, :, 128 * h : 128 * h + 128] = block
        normed[t] = normalize(state[t]).astype(BF16)
        return carry

    lax.fori_loop(0, 8, enter, 0, unroll=8)
    for load in loads[1:]:
        load.wait()
    for u in range(2):
        proj_t[u] = proj_ref[u].T
        out_proj_t[u] = out_proj_ref[u].T

    def gated(u, first, tiles):
        for t in tiles:
            p = jnp.dot(proj_t[u, first : first + 256], normed[t], preferred_element_type=F32)
            value = sigmoid(p[:128]) * p[128:]
            for h in range(2):
                staged[2 * t + h] = value[:, 128 * h : 128 * h + 128].astype(BF16)
        return jnp.swapaxes(staged[2 * tiles[0] : 2 * tiles[-1] + 2], 0, 1)

    def whole_left(u):
        send_left[...] = gated(u, 0, range(8)).reshape(8, 8, 2, 16, 128)

    def half_left(half):
        value = gated(1, 0, range(4 * half, 4 * half + 4)).astype(F32)
        send_left1[half] = value.reshape(8, 8, 16, 128).astype(BF16)

    def whole_right(u):
        send_right[u] = gated(u, 256, range(8)).reshape(8, 8, 2, 16, 128)

    def gate(u):
        def step(t, carry):
            p = jnp.dot(proj_t[u, 512:640], normed[t], preferred_element_type=F32)
            gating[t] = sigmoid(p)
            return carry

        lax.fori_loop(0, 8, step, 0, unroll=8)

    def push(src, dst, send_sem, recv_sem, device):
        pltpu.make_async_remote_copy(
            src_ref=src,
            dst_ref=dst,
            send_sem=send_sem,
            recv_sem=recv_sem,
            device_id=device,
            device_id_type=MESH,
        ).start()

    def send_all_left(src, slot, send_sem, recv_sem):
        pltpu.make_async_copy(src.at[r, q], slot, recv_sem).start()
        for dr, dq in others:
            push(src.at[rs[dr], qs[dq]], slot, send_sem, recv_sem, (rs[dr], cols[dq]))

    def send_whole_left():
        send_all_left(send_left, recv_left.at[r, q], left_send_sem.at[2], left_recv_sem.at[2])

    def send_half_left(half):
        send_all_left(
            send_left1.at[half], recv_left1.at[half, q, r], left_send_sem.at[half], left_recv_sem.at[half]
        )

    def send_all_right(u):
        slot = recv_right.at[0, r, q] if u == 0 else recv_right.at[1, q, r]
        mine = r // 2 if u == 0 else q // 2
        recv_sem = right_recv_sem.at[u, mine]
        pltpu.make_async_copy(send_right.at[u, r, q], slot, recv_sem).start()
        for t in range(4):
            pair = lax.rem(mine + 4 - t, 4) * 2
            first = r if u == 0 else q
            near = [pair + lax.rem(first + one, 2) for one in range(2)]
            for one in range(2):
                for d in range(8):
                    if t == 0 and one == 0 and d == 0:
                        continue
                    dest_r, dest_q = (near[one], qs[d]) if u == 0 else (rs[d], near[one])
                    push(
                        send_right.at[u, dest_r, dest_q],
                        slot,
                        right_send_sem.at[u],
                        recv_sem,
                        (dest_r, dest_q * 2 + core),
                    )

    def give_halves(group, values):
        for half in range(2):
            for one in range(2):
                low, high = (
                    jnp.concatenate([v[one, at : at + 8] for v in values], axis=0).astype(BF16)
                    for at in (8 * half, 8 * half + 16)
                )
                for m in range(4):
                    lanes = slice(128 * m, 128 * m + 128)
                    first, second = interleave(low[:, lanes], high[:, lanes])
                    send_half[half, 2 * group + one, 2 * m] = first
                    send_half[half, 2 * group + one, 2 * m + 1] = second

    def give_whole(group, c, value):
        for one in range(2):
            for m in range(4):
                lanes = slice(128 * m, 128 * m + 128)
                first, second = interleave(value[one, :16, lanes], value[one, 16:, lanes])
                send_whole[2 * group + one, 2 * m, c] = first
                send_whole[2 * group + one, 2 * m + 1, c] = second

    def send_back(src, slot, send_sem, recv_sem, group):
        for one in range(2):
            dest_q = 2 * group + one
            dest_col = dest_q * 2 + core
            here = dest_q == q

            @pl.when(here)
            def _():
                pltpu.make_async_copy(src.at[dest_q, r], slot, recv_sem).start()

            @pl.when(jnp.logical_not(here))
            def _():
                push(src.at[dest_q, r], slot, send_sem, recv_sem, (r, dest_col))

            for d in range(1, 8):
                push(src.at[dest_q, rs[d]], slot, send_sem, recv_sem, (rs[d], dest_col))

    def send_half_back(half, group):
        send_back(
            send_half.at[half], recv_half.at[half, chip], mixed_send_sem.at[half], mixed_recv_sem.at[half], group
        )

    def send_whole_back(group):
        send_back(send_whole, recv_whole.at[chip], mixed_send_sem.at[2], mixed_recv_sem.at[2], group)

    def wait_all(ref, sem):
        pltpu.make_async_copy(ref, ref, sem).wait()

    def outgoing():
        wait_all(recv_left, left_recv_sem.at[2])
        for c in range(2):
            for m in range(4):
                first, second = interleave(recv_left[2 * m, :, c], recv_left[2 * m + 1, :, c])
                left_op0[c, 0, :, :, 128 * m : 128 * m + 128] = first
                left_op0[c, 1, :, :, 128 * m : 128 * m + 128] = second

        def half_copy(t):
            return pltpu.make_async_remote_copy(
                src_ref=half_send.at[t],
                dst_ref=half_recv.at[t],
                send_sem=half_send_sem.at[t],
                recv_sem=half_recv_sem.at[t],
                device_id=sibling,
                device_id_type=MESH,
            )

        def finish_group(t):
            group = lax.rem(r // 2 + t, 4)
            half_copy(t).wait_recv()
            totals = [partial[t % 2, c, :, core] + half_recv[t, c].astype(F32) for c in range(2)]
            give_halves(group, totals)
            send_half_back(0, group)

        for t in range(4):
            group = lax.rem(r // 2 + t, 4)
            wait_all(recv_right.at[0, pl.ds(2 * group, 2)], right_recv_sem.at[0, group])
            for c in range(2):
                first, second = interleave(recv_right[0, 2 * group, :, c], recv_right[0, 2 * group + 1, :, c])
                right = jnp.concatenate([first.reshape(128, 128), second.reshape(128, 128)], axis=0)
                product = lax.dot_general(
                    right, left_op0[c].reshape(256, 512), (((0,), (0,)), ((), ())), preferred_element_type=F32
                )
                partial[t % 2, c] = product.reshape(2, 2, 32, 512)
                half_send[t, c] = partial[t % 2, c, :, 1 - core].astype(BF16)
            half_copy(t).start()
            if t:
                finish_group(t - 1)
        finish_group(3)
        for t in range(4):
            send_half_back(1, lax.rem(r // 2 + t, 4))
        for t in range(4):
            half_copy(t).wait_send()

    def incoming():
        def arrange(ref, half, which):
            for m in range(4):
                pieces = interleave(ref[half, :, 2 * m], ref[half, :, 2 * m + 1])
                for part in range(2):
                    for c in range(2):
                        left_op1[c, :, which, part, 8 * half : 8 * half + 8, 128 * m : 128 * m + 128] = pieces[
                            part
                        ][:, 8 * c : 8 * c + 8]

        swaps = []
        for half in range(2):
            wait_all(recv_left1.at[half], left_recv_sem.at[half])
            swap = pltpu.make_async_remote_copy(
                src_ref=recv_left1.at[half],
                dst_ref=sibling_left.at[half],
                send_sem=sib_send_sem.at[half],
                recv_sem=sib_recv_sem.at[half],
                device_id=sibling,
                device_id_type=MESH,
            )
            swap.start()
            swaps.append(swap)
            arrange(recv_left1, half, core)
        for half in range(2):
            swaps[half].wait_recv()
            arrange(sibling_left, half, 1 - core)

        for t in range(4):
            group = lax.rem(q // 2 + t, 4)
            wait_all(recv_right.at[1, pl.ds(2 * group, 2)], right_recv_sem.at[1, group])
            for c in range(2):
                columns = []
                for m in range(4):
                    even = recv_right[1, pl.ds(2 * group, 2), 2 * m, c]
                    odd = recv_right[1, pl.ds(2 * group, 2), 2 * m + 1, c]
                    columns.append(jnp.stack(interleave(even, odd), axis=1).reshape(64, 128))
                right = jnp.concatenate(columns, axis=1)
                product = lax.dot_general(
                    right, left_op1[c].reshape(512, 512), (((1,), (1,)), ((), ())), preferred_element_type=F32
                )
                give_whole(group, c, product.astype(BF16).reshape(2, 32, 512))
            send_whole_back(group)
        for swap in swaps:
            swap.wait_send()

    def absorb_half(half):
        wait_all(recv_half.at[half], mixed_recv_sem.at[half])
        norm = normalize(recv_half[half].astype(F32).reshape(128, 8, 128))
        norm = jnp.swapaxes(norm, 0, 1).astype(BF16)
        for t in range(4 * half, 4 * half + 4):
            for h in range(2):
                mixnorm[t, :, 128 * h : 128 * h + 128] = norm[2 * t + h - 8 * half]
            output = jnp.dot(out_proj_t[0], mixnorm[t], preferred_element_type=F32)
            updated = (state[t] + gating[t] * output).astype(BF16).astype(F32)
            state[t] = updated
            normed[t] = normalize(updated).astype(BF16)

    def absorb_whole():
        wait_all(recv_whole, mixed_recv_sem.at[2])
        norm = normalize(recv_whole[...].reshape(128, 16, 128).astype(F32))
        norm = jnp.swapaxes(norm.astype(BF16), 0, 1)
        for t in range(8):
            for h in range(2):
                mixnorm[t, :, 128 * h : 128 * h + 128] = norm[2 * t + h]
            output = jnp.dot(out_proj_t[1], mixnorm[t], preferred_element_type=F32)
            updated = state[t] + gating[t] * output
            for h in range(2):
                block = updated[:, 128 * h : 128 * h + 128].T.astype(BF16)
                final[:, 2 * t + h] = block.reshape(2, 64, 128)

    whole_left(0)
    pl.semaphore_wait(barrier, 64)
    send_whole_left()
    whole_right(0)
    send_all_right(0)
    gate(0)
    outgoing()
    for half in range(2):
        absorb_half(half)
        half_left(half)
        send_half_left(half)
    whole_right(1)
    send_all_right(1)
    gate(1)
    incoming()
    absorb_whole()
    out_ref[...] = final[...].reshape(32, 64, 128)

    for half in range(2):
        wait_all(recv_half.at[half, pl.ds(0, 63)], left_send_sem.at[half])
        wait_all(recv_half.at[half, pl.ds(0, 63)], mixed_send_sem.at[half])
    for sem in (left_send_sem.at[2], right_send_sem.at[0], right_send_sem.at[1], mixed_send_sem.at[2]):
        wait_all(recv_whole.at[pl.ds(0, 63)], sem)


def shards(pair_state, proj_weight, out_weight):
    vmem = pl.BlockSpec(memory_space=pltpu.VMEM)
    dma = pltpu.SemaphoreType.DMA
    out = pl.pallas_call(
        kernel,
        out_shape=jax.ShapeDtypeStruct((32, 64, 128), BF16),
        in_specs=[pl.BlockSpec(memory_space=pl.ANY)] * 3,
        out_specs=vmem,
        scratch_shapes=[
            pltpu.VMEM((64, 32, 128), BF16),
            pltpu.VMEM((2, 128, 640), BF16),
            pltpu.VMEM((2, 128, 128), BF16),
            pltpu.VMEM((2, 640, 128), BF16),
            pltpu.VMEM((2, 128, 128), BF16),
            pltpu.VMEM((8, 128, 256), F32),
            pltpu.VMEM((8, 128, 256), BF16),
            pltpu.VMEM((8, 128, 256), F32),
            pltpu.VMEM((16, 128, 128), BF16),
            pltpu.VMEM((8, 128, 256), BF16),
            pltpu.VMEM((2, 16, 64, 128), BF16),
            pltpu.VMEM((2, 2, 8, 16, 512), BF16),
            pltpu.VMEM((2, 8, 2, 2, 16, 512), BF16),
            pltpu.VMEM((2, 2, 2, 2, 32, 512), F32),
            pltpu.VMEM((8, 8, 2, 16, 128), BF16),
            pltpu.VMEM((2, 8, 8, 16, 128), BF16),
            pltpu.VMEM((2, 8, 8, 2, 16, 128), BF16),
            pltpu.VMEM((8, 8, 2, 16, 128), BF16),
            pltpu.VMEM((2, 8, 8, 16, 128), BF16),
            pltpu.VMEM((2, 8, 8, 2, 16, 128), BF16),
            pltpu.VMEM((2, 8, 8, 16, 128), BF16),
            pltpu.VMEM((4, 2, 2, 32, 512), BF16),
            pltpu.VMEM((4, 2, 2, 32, 512), BF16),
            pltpu.VMEM((2, 8, 8, 16, 128), BF16),
            pltpu.VMEM((2, 64, 16, 128), BF16),
            pltpu.VMEM((8, 8, 2, 16, 128), BF16),
            pltpu.VMEM((64, 2, 16, 128), BF16),
            dma((3,)),
            dma((3,)),
            dma((2,)),
            dma((2, 4)),
            dma((2,)),
            dma((2,)),
            dma((4,)),
            dma((4,)),
            dma((3,)),
            dma((3,)),
            dma((3,)),
        ],
        compiler_params=pltpu.CompilerParams(
            collective_id=0, has_side_effects=True, vmem_limit_bytes=56 * 2**20
        ),
    )(pair_state, proj_weight, out_weight)
    return jnp.transpose(out, (1, 0, 2))


def solution(mesh):
    in_specs = (P("row", "col", None), P(), P())
    out_specs = P("row", "col", None)
    return jax.shard_map(shards, mesh=mesh, in_specs=in_specs, out_specs=out_specs, check_vma=False)
```

```python
import functools

import jax
import jax.numpy as jnp
from jax import lax
from jax.experimental import pallas as pl
from jax.experimental.pallas import tpu as pltpu
from jax.sharding import PartitionSpec as P

F32 = jnp.float32
BF16 = jnp.bfloat16
MESH = pl.DeviceIdType.MESH


def sigmoid(x):
    return 0.5 * jnp.tanh(0.5 * x) + 0.5


def normalize(x):
    center = x - jnp.mean(x, axis=0, keepdims=True)
    spread = jnp.mean(center * center, axis=0, keepdims=True)
    return center * lax.rsqrt(spread + 1e-05)


def interleave(even, odd):
    first = jnp.concatenate([even[..., :64], odd[..., :64]], axis=-1)
    second = jnp.concatenate([even[..., 64:], odd[..., 64:]], axis=-1)
    return first, second


def kernel(
    pair_hbm,
    proj_hbm,
    out_proj_hbm,
    out_ref,
    pair_ref,
    proj_ref,
    out_proj_ref,
    proj_t,
    out_proj_t,
    state,
    normed,
    gating,
    staged,
    mixnorm,
    final,
    left_op0,
    left_op1,
    partial,
    send_left,
    send_left1,
    send_right,
    recv_left,
    recv_left1,
    recv_right,
    sibling_left,
    half_send,
    half_recv,
    send_half,
    recv_half,
    send_whole,
    recv_whole,
    left_send_sem,
    left_recv_sem,
    right_send_sem,
    right_recv_sem,
    sib_send_sem,
    sib_recv_sem,
    half_send_sem,
    half_recv_sem,
    mixed_send_sem,
    mixed_recv_sem,
    load_sem,
    out_sem,
):
    r = lax.axis_index("row")
    col = lax.axis_index("col")
    q = col // 2
    core = col % 2
    chip = r * 8 + q

    def around(place):
        return [lax.rem(place // 4 + d // 4, 2) * 4 + lax.rem(place % 4 + d % 4, 4) for d in range(8)]

    rs, qs = around(r), around(q)

    def group_of(place):
        return place // 4 * 2 + place % 2

    def place_of(group, one):
        return group // 2 * 4 + group % 2 + 2 * one

    start = lax.rem(r % 4 + q // 4 * 2 + q % 4, 4)
    turns = [lax.rem(start + t, 4) for t in range(4)]
    cols = [dest_q * 2 + core for dest_q in qs]
    sibling = (r, q * 2 + 1 - core)
    others = [(d // 8, d % 8) for d in sorted(range(1,64), key=lambda e: (e * 7919) % 1009)]

    loads = [
        pltpu.make_async_copy(src, dst, load_sem.at[i])
        for i, (src, dst) in enumerate(
            ((pair_hbm, pair_ref), (proj_hbm, proj_ref), (out_proj_hbm, out_proj_ref))
        )
    ]
    for load in loads:
        load.start()

    barrier = pltpu.get_barrier_semaphore()

    for dr, dq in others:
        pl.semaphore_signal(barrier, inc=1, device_id=(rs[dr], cols[dq]), device_id_type=MESH)
    pl.semaphore_signal(barrier, inc=1, device_id=sibling, device_id_type=MESH)

    loads[0].wait()
    pair = jnp.swapaxes(pair_ref[...], 0, 1)
    final[...] = pair.reshape(2, 16, 64, 128)

    def enter(t, carry):
        for h in range(2):
            block = final[:, 2 * t + h].reshape(128, 128).astype(F32).T
            state[t, :, 128 * h : 128 * h + 128] = block
        normed[t] = normalize(state[t]).astype(BF16)
        return carry

    lax.fori_loop(0, 8, enter, 0, unroll=8)
    for load in loads[1:]:
        load.wait()
    for u in range(2):
        proj_t[u] = proj_ref[u].T
        out_proj_t[u] = out_proj_ref[u].T

    def gated(u, first, tiles):
        for t in tiles:
            p = jnp.dot(proj_t[u, first : first + 256], normed[t], preferred_element_type=F32)
            value = sigmoid(p[:128]) * p[128:]
            for h in range(2):
                staged[2 * t + h] = value[:, 128 * h : 128 * h + 128].astype(BF16)
        return jnp.swapaxes(staged[2 * tiles[0] : 2 * tiles[-1] + 2], 0, 1)

    def whole_left(u):
        send_left[...] = gated(u, 0, range(8)).reshape(8, 8, 2, 16, 128)

    def half_left(half):
        value = gated(1, 0, range(4 * half, 4 * half + 4)).astype(F32)
        send_left1[half] = value.reshape(8, 8, 16, 128).astype(BF16)

    def whole_right(u):
        send_right[u] = gated(u, 256, range(8)).reshape(8, 8, 2, 16, 128)

    def gate(u):
        def step(t, carry):
            p = jnp.dot(proj_t[u, 512:640], normed[t], preferred_element_type=F32)
            gating[t] = sigmoid(p)
            return carry

        lax.fori_loop(0, 8, step, 0, unroll=8)

    def push(src, dst, send_sem, recv_sem, device):
        pltpu.make_async_remote_copy(
            src_ref=src,
            dst_ref=dst,
            send_sem=send_sem,
            recv_sem=recv_sem,
            device_id=device,
            device_id_type=MESH,
        ).start()

    def send_all_left(src, slot, send_sem, recv_sem):
        pltpu.make_async_copy(src.at[r, q], slot, recv_sem).start()
        for dr, dq in others:
            push(src.at[rs[dr], qs[dq]], slot, send_sem, recv_sem, (rs[dr], cols[dq]))

    def send_whole_left():
        send_all_left(send_left, recv_left.at[r, q], left_send_sem.at[2], left_recv_sem.at[2])

    def send_half_left(half):
        send_all_left(
            send_left1.at[half], recv_left1.at[half, q, r], left_send_sem.at[half], left_recv_sem.at[half]
        )

    def send_all_right(u):
        place, other = (r, q) if u == 0 else (q, r)
        mine = group_of(place)
        slot = recv_right.at[u, mine, place % 4 // 2, other]
        send_sem, recv_sem = right_send_sem.at[u], right_recv_sem.at[u, mine]
        for t in range(4):
            for dz in range(2):
                dest_rz = rs[4 * dz] // 4 * 4
                for d in range(8):
                    dest_q = qs[d]
                    dest_r = dest_rz + lax.rem(mine + 16 - t - dest_q // 4 * 2 - dest_q % 4, 4)
                    src = send_right.at[u, dest_r, dest_q]
                    if dz or d:
                        push(src, slot, send_sem, recv_sem, (dest_r, cols[d]))
                        continue
                    here = dest_r == r

                    @pl.when(here)
                    def _():
                        pltpu.make_async_copy(src, slot, recv_sem).start()

                    @pl.when(jnp.logical_not(here))
                    def _():
                        push(src, slot, send_sem, recv_sem, (dest_r, cols[d]))

    def give_halves(group, values):
        for half in range(2):
            for one in range(2):
                low, high = (
                    jnp.concatenate([v[one, at : at + 8] for v in values], axis=0).astype(BF16)
                    for at in (8 * half, 8 * half + 16)
                )
                for m in range(4):
                    lanes = slice(128 * m, 128 * m + 128)
                    first, second = interleave(low[:, lanes], high[:, lanes])
                    send_half[half, place_of(group, one), 2 * m] = first
                    send_half[half, place_of(group, one), 2 * m + 1] = second

    def give_whole(group, c, value):
        for one in range(2):
            for m in range(4):
                lanes = slice(128 * m, 128 * m + 128)
                first, second = interleave(value[one, :16, lanes], value[one, 16:, lanes])
                send_whole[place_of(group, one), 2 * m, c] = first
                send_whole[place_of(group, one), 2 * m + 1, c] = second

    def send_back(src, slot, send_sem, recv_sem, group):
        for one in range(2):
            dest_q = place_of(group, one)
            dest_col = dest_q * 2 + core
            here = dest_q == q

            @pl.when(here)
            def _():
                pltpu.make_async_copy(src.at[dest_q, r], slot, recv_sem).start()

            @pl.when(jnp.logical_not(here))
            def _():
                push(src.at[dest_q, r], slot, send_sem, recv_sem, (r, dest_col))

            for d in range(1, 8):
                push(src.at[dest_q, rs[d]], slot, send_sem, recv_sem, (rs[d], dest_col))

    def send_half_back(half, group):
        send_back(
            send_half.at[half], recv_half.at[half, chip], mixed_send_sem.at[half], mixed_recv_sem.at[half], group
        )

    def send_whole_back(group):
        send_back(send_whole, recv_whole.at[chip], mixed_send_sem.at[2], mixed_recv_sem.at[2], group)

    def wait_all(ref, sem):
        pltpu.make_async_copy(ref, ref, sem).wait()

    def outgoing():
        wait_all(recv_left, left_recv_sem.at[2])
        for c in range(2):
            for m in range(4):
                first, second = interleave(recv_left[2 * m, :, c], recv_left[2 * m + 1, :, c])
                left_op0[c, 0, :, :, 128 * m : 128 * m + 128] = first
                left_op0[c, 1, :, :, 128 * m : 128 * m + 128] = second

        def half_copy(t):
            return pltpu.make_async_remote_copy(
                src_ref=half_send.at[t],
                dst_ref=half_recv.at[t],
                send_sem=half_send_sem.at[t],
                recv_sem=half_recv_sem.at[t],
                device_id=sibling,
                device_id_type=MESH,
            )

        def finish_group(t):
            group = turns[t]
            half_copy(t).wait_recv()
            totals = [partial[t % 2, c, :, core] + half_recv[t, c].astype(F32) for c in range(2)]
            give_halves(group, totals)
            send_half_back(0, group)

        for t in range(4):
            group = turns[t]
            wait_all(recv_right.at[0, group], right_recv_sem.at[0, group])
            for c in range(2):
                first, second = interleave(recv_right[0, group, 0, :, c], recv_right[0, group, 1, :, c])
                right = jnp.concatenate([first.reshape(128, 128), second.reshape(128, 128)], axis=0)
                product = lax.dot_general(
                    right, left_op0[c].reshape(256, 512), (((0,), (0,)), ((), ())), preferred_element_type=F32
                )
                partial[t % 2, c] = product.reshape(2, 2, 32, 512)
                half_send[t, c] = partial[t % 2, c, :, 1 - core].astype(BF16)
            half_copy(t).start()
            if t:
                finish_group(t - 1)
        finish_group(3)
        for t in range(4):
            send_half_back(1, turns[t])
        for t in range(4):
            half_copy(t).wait_send()

    def incoming():
        def arrange(ref, half, which):
            for m in range(4):
                pieces = interleave(ref[half, :, 2 * m], ref[half, :, 2 * m + 1])
                for part in range(2):
                    for c in range(2):
                        left_op1[c, :, which, part, 8 * half : 8 * half + 8, 128 * m : 128 * m + 128] = pieces[
                            part
                        ][:, 8 * c : 8 * c + 8]

        swaps = []
        for half in range(2):
            wait_all(recv_left1.at[half], left_recv_sem.at[half])
            swap = pltpu.make_async_remote_copy(
                src_ref=recv_left1.at[half],
                dst_ref=sibling_left.at[half],
                send_sem=sib_send_sem.at[half],
                recv_sem=sib_recv_sem.at[half],
                device_id=sibling,
                device_id_type=MESH,
            )
            swap.start()
            swaps.append(swap)
            arrange(recv_left1, half, core)
        for half in range(2):
            swaps[half].wait_recv()
            arrange(sibling_left, half, 1 - core)

        for t in range(4):
            group = turns[t]
            wait_all(recv_right.at[1, group], right_recv_sem.at[1, group])
            for c in range(2):
                columns = []
                for m in range(4):
                    even = recv_right[1, group, :, 2 * m, c]
                    odd = recv_right[1, group, :, 2 * m + 1, c]
                    columns.append(jnp.stack(interleave(even, odd), axis=1).reshape(64, 128))
                right = jnp.concatenate(columns, axis=1)
                product = lax.dot_general(
                    right, left_op1[c].reshape(512, 512), (((1,), (1,)), ((), ())), preferred_element_type=F32
                )
                give_whole(group, c, product.astype(BF16).reshape(2, 32, 512))
            send_whole_back(group)
        for swap in swaps:
            swap.wait_send()

    def absorb_half(half):
        wait_all(recv_half.at[half], mixed_recv_sem.at[half])
        norm = normalize(recv_half[half].astype(F32).reshape(128, 8, 128))
        norm = jnp.swapaxes(norm, 0, 1).astype(BF16)
        for t in range(4 * half, 4 * half + 4):
            for h in range(2):
                mixnorm[t, :, 128 * h : 128 * h + 128] = norm[2 * t + h - 8 * half]
            output = jnp.dot(out_proj_t[0], mixnorm[t], preferred_element_type=F32)
            updated = (state[t] + gating[t] * output).astype(BF16).astype(F32)
            state[t] = updated
            normed[t] = normalize(updated).astype(BF16)

    def absorb_whole():
        wait_all(recv_whole, mixed_recv_sem.at[2])
        norm = normalize(recv_whole[...].reshape(128, 16, 128).astype(F32))
        norm = jnp.swapaxes(norm.astype(BF16), 0, 1)
        for t in range(8):
            for h in range(2):
                mixnorm[t, :, 128 * h : 128 * h + 128] = norm[2 * t + h]
            output = jnp.dot(out_proj_t[1], mixnorm[t], preferred_element_type=F32)
            updated = state[t] + gating[t] * output
            for h in range(2):
                block = updated[:, 128 * h : 128 * h + 128].T.astype(BF16)
                final[:, 2 * t + h] = block.reshape(2, 64, 128)
            for part in range(2):
                pltpu.make_async_copy(
                    final.at[part, pl.ds(2 * t, 2)], out_ref.at[pl.ds(16 * part + 2 * t, 2)], out_sem
                ).start()

    whole_left(0)
    pl.semaphore_wait(barrier, 64)
    send_whole_left()
    whole_right(0)
    send_all_right(0)
    gate(0)
    outgoing()
    for half in range(2):
        absorb_half(half)
        half_left(half)
        send_half_left(half)
    whole_right(1)
    send_all_right(1)
    gate(1)
    incoming()
    absorb_whole()

    for half in range(2):
        wait_all(recv_half.at[half, pl.ds(0, 63)], left_send_sem.at[half])
        wait_all(recv_half.at[half, pl.ds(0, 63)], mixed_send_sem.at[half])
    for sem in (left_send_sem.at[2], right_send_sem.at[0], right_send_sem.at[1], mixed_send_sem.at[2]):
        wait_all(recv_whole.at[pl.ds(0, 63)], sem)
    wait_all(out_ref, out_sem)


def shards(pair_state, proj_weight, out_weight):
    dma = pltpu.SemaphoreType.DMA
    out = pl.pallas_call(
        kernel,
        out_shape=jax.ShapeDtypeStruct((32, 64, 128), BF16),
        in_specs=[pl.BlockSpec(memory_space=pl.ANY)] * 3,
        out_specs=pl.BlockSpec(memory_space=pl.ANY),
        scratch_shapes=[
            pltpu.VMEM((64, 32, 128), BF16),
            pltpu.VMEM((2, 128, 640), BF16),
            pltpu.VMEM((2, 128, 128), BF16),
            pltpu.VMEM((2, 640, 128), BF16),
            pltpu.VMEM((2, 128, 128), BF16),
            pltpu.VMEM((8, 128, 256), F32),
            pltpu.VMEM((8, 128, 256), BF16),
            pltpu.VMEM((8, 128, 256), F32),
            pltpu.VMEM((16, 128, 128), BF16),
            pltpu.VMEM((8, 128, 256), BF16),
            pltpu.VMEM((2, 16, 64, 128), BF16),
            pltpu.VMEM((2, 2, 8, 16, 512), BF16),
            pltpu.VMEM((2, 8, 2, 2, 16, 512), BF16),
            pltpu.VMEM((2, 2, 2, 2, 32, 512), F32),
            pltpu.VMEM((8, 8, 2, 16, 128), BF16),
            pltpu.VMEM((2, 8, 8, 16, 128), BF16),
            pltpu.VMEM((2, 8, 8, 2, 16, 128), BF16),
            pltpu.VMEM((8, 8, 2, 16, 128), BF16),
            pltpu.VMEM((2, 8, 8, 16, 128), BF16),
            pltpu.VMEM((2, 4, 2, 8, 2, 16, 128), BF16),
            pltpu.VMEM((2, 8, 8, 16, 128), BF16),
            pltpu.VMEM((4, 2, 2, 32, 512), BF16),
            pltpu.VMEM((4, 2, 2, 32, 512), BF16),
            pltpu.VMEM((2, 8, 8, 16, 128), BF16),
            pltpu.VMEM((2, 64, 16, 128), BF16),
            pltpu.VMEM((8, 8, 2, 16, 128), BF16),
            pltpu.VMEM((64, 2, 16, 128), BF16),
            dma((3,)),
            dma((3,)),
            dma((2,)),
            dma((2, 4)),
            dma((2,)),
            dma((2,)),
            dma((4,)),
            dma((4,)),
            dma((3,)),
            dma((3,)),
            dma((3,)),
            dma,
        ],
        compiler_params=pltpu.CompilerParams(
            collective_id=0, has_side_effects=True, vmem_limit_bytes=56 * 2**20
        ),
    )(pair_state, proj_weight, out_weight)
    return jnp.transpose(out, (1, 0, 2))


def solution(mesh):
    in_specs = (P("row", "col", None), P(), P())
    out_specs = P("row", "col", None)
    return jax.shard_map(shards, mesh=mesh, in_specs=in_specs, out_specs=out_specs, check_vma=False)
```

```python
import functools

import jax
import jax.numpy as jnp
from jax import lax
from jax.experimental import pallas as pl
from jax.experimental.pallas import tpu as pltpu
from jax.sharding import PartitionSpec as P

F32 = jnp.float32
BF16 = jnp.bfloat16
MESH = pl.DeviceIdType.MESH


def sigmoid(x):
    return 0.5 * jnp.tanh(0.5 * x) + 0.5


def normalize(x):
    center = x - jnp.mean(x, axis=0, keepdims=True)
    spread = jnp.mean(center * center, axis=0, keepdims=True)
    return center * lax.rsqrt(spread + 1e-05)


def interleave(even, odd):
    first = jnp.concatenate([even[..., :64], odd[..., :64]], axis=-1)
    second = jnp.concatenate([even[..., 64:], odd[..., 64:]], axis=-1)
    return first, second


def swap_blocks(x, axis):
    blocks = jnp.split(x, 4, axis=axis)
    return jnp.concatenate([blocks[0], blocks[2], blocks[1], blocks[3]], axis=axis)


def kernel(
    pair_hbm,
    proj_hbm,
    out_proj_hbm,
    out_ref,
    pair_ref,
    proj_ref,
    out_proj_ref,
    proj_t,
    out_proj_t,
    state,
    normed,
    gating,
    staged,
    mixnorm,
    final,
    left_op0,
    left_op1,
    partial,
    send_left,
    send_left1,
    send_right0,
    send_right,
    recv_left,
    recv_left1,
    recv_right0,
    recv_right,
    right_op,
    sibling_left,
    half_send,
    half_recv,
    send_half,
    recv_half,
    send_whole,
    recv_whole,
    left_send_sem,
    left_recv_sem,
    right_send_sem,
    right_recv0_sem,
    right_recv_sem,
    sib_send_sem,
    sib_recv_sem,
    half_send_sem,
    half_recv_sem,
    mixed_send_sem,
    mixed_recv_sem,
    load_sem,
    out_sem,
):
    r = lax.axis_index("row")
    col = lax.axis_index("col")
    q = col // 2
    core = col % 2
    chip = r * 8 + q

    def around(place):
        return [lax.rem(place // 4 + d // 4, 2) * 4 + lax.rem(place % 4 + d % 4, 4) for d in range(8)]

    rs, qs = around(r), around(q)

    def group_of(place):
        return place // 4 * 2 + place % 2

    def place_of(group, one):
        return group // 2 * 4 + group % 2 + 2 * one

    start = lax.rem(r % 4 + q // 4 * 2 + q % 4, 4)
    turns = [lax.rem(start + t, 4) for t in range(4)]

    sets = [lax.rem(r + q + t, 2) for t in range(2)]
    cols = [dest_q * 2 + core for dest_q in qs]
    sibling = (r, q * 2 + 1 - core)
    others = [(d // 8, d % 8) for d in sorted(range(1,64), key=lambda e: (e * 7919) % 1009)]

    loads = [
        pltpu.make_async_copy(src, dst, load_sem.at[i])
        for i, (src, dst) in enumerate(
            ((pair_hbm, pair_ref), (proj_hbm, proj_ref), (out_proj_hbm, out_proj_ref))
        )
    ]
    for load in loads:
        load.start()

    barrier = pltpu.get_barrier_semaphore()

    for dr, dq in others:
        pl.semaphore_signal(barrier, inc=1, device_id=(rs[dr], cols[dq]), device_id_type=MESH)
    pl.semaphore_signal(barrier, inc=1, device_id=sibling, device_id_type=MESH)

    loads[0].wait()
    pair = jnp.swapaxes(swap_blocks(pair_ref[...], 0), 0, 1)
    for half in range(2):
        for part in range(2):
            first = 16 * half + 8 * part
            final[part, 8 * half : 8 * half + 8] = pair[first : first + 8]

    def enter(t, carry):
        for h in range(2):
            block = final[:, 2 * t + h].reshape(128, 128).astype(F32).T
            state[t, :, 128 * h : 128 * h + 128] = block
        normed[t] = normalize(state[t]).astype(BF16)
        return carry

    lax.fori_loop(0, 8, enter, 0, unroll=8)
    for load in loads[1:]:
        load.wait()
    for u in range(2):
        proj_t[u] = proj_ref[u].T
        out_proj_t[u] = out_proj_ref[u].T

    def gated(u, first, tiles):
        for t in tiles:
            p = jnp.dot(proj_t[u, first : first + 256], normed[t], preferred_element_type=F32)
            value = sigmoid(p[:128]) * p[128:]
            for h in range(2):
                staged[2 * t + h] = value[:, 128 * h : 128 * h + 128].astype(BF16)
        return jnp.swapaxes(staged[2 * tiles[0] : 2 * tiles[-1] + 2], 0, 1)

    def whole_left(u):
        send_left[...] = gated(u, 0, range(8)).reshape(8, 8, 2, 16, 128)

    def half_left(half):
        value = gated(1, 0, range(4 * half, 4 * half + 4)).astype(F32)
        send_left1[half] = value.reshape(8, 8, 16, 128).astype(BF16)

    def half_rights():
        value = gated(0, 256, range(8)).astype(F32)
        low, high = value[:, :8], value[:, 8:]
        for half in range(2):
            lanes = [slice(32 * half + 64 * part, 32 * half + 64 * part + 32) for part in range(2)]
            pieces = jnp.concatenate([tile[..., at] for tile in (low, high) for at in lanes], axis=-1)
            send_right0[half] = pieces.reshape(8, 8, 16, 128).astype(BF16)

    def whole_right():
        send_right[...] = gated(1, 256, range(8)).reshape(8, 8, 2, 16, 128)

    def gate(u):
        def step(t, carry):
            p = jnp.dot(proj_t[u, 512:640], normed[t], preferred_element_type=F32)
            gating[t] = sigmoid(p)
            return carry

        lax.fori_loop(0, 8, step, 0, unroll=8)

    def push(src, dst, send_sem, recv_sem, device):
        pltpu.make_async_remote_copy(
            src_ref=src,
            dst_ref=dst,
            send_sem=send_sem,
            recv_sem=recv_sem,
            device_id=device,
            device_id_type=MESH,
        ).start()

    def push_or_keep(here, src, dst, send_sem, recv_sem, device):
        @pl.when(here)
        def _():
            pltpu.make_async_copy(src, dst, recv_sem).start()

        @pl.when(jnp.logical_not(here))
        def _():
            push(src, dst, send_sem, recv_sem, device)

    def send_all_left(src, slot, send_sem, recv_sem):
        pltpu.make_async_copy(src.at[r, q], slot, recv_sem).start()
        for dr, dq in others:
            push(src.at[rs[dr], qs[dq]], slot, send_sem, recv_sem, (rs[dr], cols[dq]))

    def send_whole_left():
        send_all_left(send_left, recv_left.at[r, q], left_send_sem.at[2], left_recv_sem.at[2])

    def send_half_left(half):
        send_all_left(
            send_left1.at[half], recv_left1.at[half, q, r], left_send_sem.at[half], left_recv_sem.at[half]
        )

    def send_half_right(half):
        mine = r % 2
        slot = recv_right0.at[half, mine, r // 2, q]
        send_sem, recv_sem = right_send_sem.at[half], right_recv0_sem.at[half, mine]
        for t in range(2):
            for d in range(32):
                dest_q = qs[d % 8]
                dest_r = lax.rem(r // 2 + d // 8, 4) * 2 + lax.rem(mine + t + dest_q, 2)
                col = cols[d % 8]
                src = send_right0.at[half, dest_r, dest_q]
                if d:
                    push(src, slot, send_sem, recv_sem, (dest_r, col))
                else:
                    push_or_keep(dest_r == r, src, slot, send_sem, recv_sem, (dest_r, col))

    def send_whole_right():
        mine = group_of(q)
        slot = recv_right.at[mine, q % 4 // 2, r]
        send_sem, recv_sem = right_send_sem.at[2], right_recv_sem.at[mine]
        for t in range(4):
            for dz in range(2):
                dest_rz = rs[4 * dz] // 4 * 4
                for d in range(8):
                    dest_q = qs[d]
                    dest_r = dest_rz + lax.rem(mine + 16 - t - dest_q // 4 * 2 - dest_q % 4, 4)
                    src = send_right.at[dest_r, dest_q]
                    if dz or d:
                        push(src, slot, send_sem, recv_sem, (dest_r, cols[d]))
                    else:
                        push_or_keep(dest_r == r, src, slot, send_sem, recv_sem, (dest_r, cols[d]))

    def give_half(half, members, values):
        for one, dest_q in enumerate(members):
            low, high = (
                jnp.concatenate([v[one, at : at + 8] for v in values], axis=0).astype(BF16) for at in (0, 8)
            )
            for m in range(4):
                lanes = slice(128 * m, 128 * m + 128)
                first, second = interleave(low[:, lanes], high[:, lanes])
                send_half[half, dest_q, 2 * m] = first
                send_half[half, dest_q, 2 * m + 1] = second

    def give_whole(group, c, value):
        for one in range(2):
            for m in range(4):
                lanes = slice(128 * m, 128 * m + 128)
                first, second = interleave(value[one, :16, lanes], value[one, 16:, lanes])
                send_whole[place_of(group, one), 2 * m, c] = first
                send_whole[place_of(group, one), 2 * m + 1, c] = second

    def send_back(src, slot, send_sem, recv_sem, members):
        for dest_q in members:
            dest_col = dest_q * 2 + core
            push_or_keep(dest_q == q, src.at[dest_q, r], slot, send_sem, recv_sem, (r, dest_col))
            for d in range(1, 8):
                push(src.at[dest_q, rs[d]], slot, send_sem, recv_sem, (rs[d], dest_col))

    def send_half_back(half, members):
        send_back(
            send_half.at[half], recv_half.at[half, chip], mixed_send_sem.at[half], mixed_recv_sem.at[half], members
        )

    def send_whole_back(group):
        members = [place_of(group, one) for one in range(2)]
        send_back(send_whole, recv_whole.at[chip], mixed_send_sem.at[2], mixed_recv_sem.at[2], members)

    def wait_all(ref, sem):
        pltpu.make_async_copy(ref, ref, sem).wait()

    def outgoing():
        wait_all(recv_left, left_recv_sem.at[2])
        for c in range(2):
            for m in range(4):
                first, second = interleave(recv_left[2 * m, :, c], recv_left[2 * m + 1, :, c])
                left_op0[c, 0, :, :, 128 * m : 128 * m + 128] = first
                left_op0[c, 1, :, :, 128 * m : 128 * m + 128] = second

        def half_copy(t):
            return pltpu.make_async_remote_copy(
                src_ref=half_send.at[t],
                dst_ref=half_recv.at[t],
                send_sem=half_send_sem.at[t],
                recv_sem=half_recv_sem.at[t],
                device_id=sibling,
                device_id_type=MESH,
            )

        def members_of(t):
            return [2 * one + sets[t % 2] for one in range(4)]

        def finish(t):
            half_copy(t).wait_recv()
            totals = [partial[t % 2, c, :, core] + half_recv[t, c].astype(F32) for c in range(2)]
            give_half(t // 2, members_of(t), totals)
            send_half_back(t // 2, members_of(t))

        for t in range(4):
            half, which = t // 2, sets[t % 2]
            wait_all(recv_right0.at[half, which], right_recv0_sem.at[half, which])
            for piece in range(4):
                lanes = slice(32 * piece, 32 * piece + 32)
                block = jnp.concatenate([recv_right0[half, which, one, :, :, lanes] for one in range(4)], axis=-1)
                high, part = piece // 2, piece % 2
                for c in range(2):
                    right_op[c, part, :, 8 * high : 8 * high + 8] = block[:, 8 * c : 8 * c + 8]
            for c in range(2):
                product = lax.dot_general(
                    right_op[c].reshape(256, 128),
                    left_op0[c].reshape(256, 512),
                    (((0,), (0,)), ((), ())),
                    preferred_element_type=F32,
                )
                partial[t % 2, c] = product.reshape(4, 2, 16, 512)
                half_send[t, c] = partial[t % 2, c, :, 1 - core].astype(BF16)
            half_copy(t).start()
            if t:
                finish(t - 1)
        finish(3)
        for t in range(4):
            half_copy(t).wait_send()

    def incoming():
        def arrange(ref, half, which):
            for m in range(4):
                pieces = interleave(ref[half, :, 2 * m], ref[half, :, 2 * m + 1])
                for part in range(2):
                    for c in range(2):
                        left_op1[c, :, half, which, 8 * part : 8 * part + 8, 128 * m : 128 * m + 128] = pieces[
                            part
                        ][:, 8 * c : 8 * c + 8]

        swaps = []
        for half in range(2):
            wait_all(recv_left1.at[half], left_recv_sem.at[half])
            swap = pltpu.make_async_remote_copy(
                src_ref=recv_left1.at[half],
                dst_ref=sibling_left.at[half],
                send_sem=sib_send_sem.at[half],
                recv_sem=sib_recv_sem.at[half],
                device_id=sibling,
                device_id_type=MESH,
            )
            swap.start()
            swaps.append(swap)
            arrange(recv_left1, half, core)
        for half in range(2):
            swaps[half].wait_recv()
            arrange(sibling_left, half, 1 - core)

        for t in range(4):
            group = turns[t]
            wait_all(recv_right.at[group], right_recv_sem.at[group])
            for c in range(2):
                columns = []
                for m in range(4):
                    even = recv_right[group, :, 2 * m, c]
                    odd = recv_right[group, :, 2 * m + 1, c]
                    columns.append(jnp.stack(interleave(even, odd), axis=1).reshape(64, 128))
                right = jnp.concatenate(columns, axis=1)
                product = lax.dot_general(
                    right, left_op1[c].reshape(512, 512), (((1,), (1,)), ((), ())), preferred_element_type=F32
                )
                give_whole(group, c, product.astype(BF16).reshape(2, 32, 512))
            send_whole_back(group)
        for swap in swaps:
            swap.wait_send()

    def absorb_half(half):
        wait_all(recv_half.at[half], mixed_recv_sem.at[half])
        norm = normalize(recv_half[half].astype(F32).reshape(128, 8, 128))
        norm = jnp.swapaxes(norm, 0, 1).astype(BF16)
        for t in range(4 * half, 4 * half + 4):
            for h in range(2):
                mixnorm[t, :, 128 * h : 128 * h + 128] = norm[2 * t + h - 8 * half]
            output = jnp.dot(out_proj_t[0], mixnorm[t], preferred_element_type=F32)
            updated = (state[t] + gating[t] * output).astype(BF16).astype(F32)
            state[t] = updated
            normed[t] = normalize(updated).astype(BF16)

    def absorb_whole():
        wait_all(recv_whole, mixed_recv_sem.at[2])
        norm = normalize(recv_whole[...].reshape(128, 16, 128).astype(F32))
        norm = jnp.swapaxes(norm.astype(BF16), 0, 1)
        for t in range(8):
            for h in range(2):
                mixnorm[t, :, 128 * h : 128 * h + 128] = norm[2 * t + h]
            output = jnp.dot(out_proj_t[1], mixnorm[t], preferred_element_type=F32)
            updated = state[t] + gating[t] * output
            for h in range(2):
                block = updated[:, 128 * h : 128 * h + 128].T.astype(BF16)
                final[:, 2 * t + h] = swap_blocks(block.reshape(2, 64, 128), 1)
            for part in range(2):
                column = 16 * (t // 4) + 8 * part + 2 * t % 8
                pltpu.make_async_copy(
                    final.at[part, pl.ds(2 * t, 2)], out_ref.at[pl.ds(column, 2)], out_sem
                ).start()

    whole_left(0)
    pl.semaphore_wait(barrier, 64)
    send_whole_left()
    half_rights()
    for half in range(2):
        send_half_right(half)
    gate(0)
    outgoing()
    for half in range(2):
        absorb_half(half)
        half_left(half)
        send_half_left(half)
    whole_right()
    send_whole_right()
    gate(1)
    incoming()
    absorb_whole()

    for half in range(2):
        wait_all(recv_half.at[half, pl.ds(0, 63)], left_send_sem.at[half])
        wait_all(recv_half.at[half, pl.ds(0, 63)], right_send_sem.at[half])
        wait_all(recv_half.at[half, pl.ds(0, 63)], mixed_send_sem.at[half])
    for sem in (left_send_sem.at[2], right_send_sem.at[2], mixed_send_sem.at[2]):
        wait_all(recv_whole.at[pl.ds(0, 63)], sem)
    wait_all(out_ref, out_sem)


def shards(pair_state, proj_weight, out_weight):
    dma = pltpu.SemaphoreType.DMA
    out = pl.pallas_call(
        kernel,
        out_shape=jax.ShapeDtypeStruct((32, 64, 128), BF16),
        in_specs=[pl.BlockSpec(memory_space=pl.ANY)] * 3,
        out_specs=pl.BlockSpec(memory_space=pl.ANY),
        scratch_shapes=[
            pltpu.VMEM((64, 32, 128), BF16),
            pltpu.VMEM((2, 128, 640), BF16),
            pltpu.VMEM((2, 128, 128), BF16),
            pltpu.VMEM((2, 640, 128), BF16),
            pltpu.VMEM((2, 128, 128), BF16),
            pltpu.VMEM((8, 128, 256), F32),
            pltpu.VMEM((8, 128, 256), BF16),
            pltpu.VMEM((8, 128, 256), F32),
            pltpu.VMEM((16, 128, 128), BF16),
            pltpu.VMEM((8, 128, 256), BF16),
            pltpu.VMEM((2, 16, 64, 128), BF16),
            pltpu.VMEM((2, 2, 8, 16, 512), BF16),
            pltpu.VMEM((2, 8, 2, 2, 16, 512), BF16),
            pltpu.VMEM((2, 2, 4, 2, 16, 512), F32),
            pltpu.VMEM((8, 8, 2, 16, 128), BF16),
            pltpu.VMEM((2, 8, 8, 16, 128), BF16),
            pltpu.VMEM((2, 8, 8, 16, 128), BF16),
            pltpu.VMEM((8, 8, 2, 16, 128), BF16),
            pltpu.VMEM((8, 8, 2, 16, 128), BF16),
            pltpu.VMEM((2, 8, 8, 16, 128), BF16),
            pltpu.VMEM((2, 2, 4, 8, 16, 128), BF16),
            pltpu.VMEM((4, 2, 8, 2, 16, 128), BF16),
            pltpu.VMEM((2, 2, 8, 16, 128), BF16),
            pltpu.VMEM((2, 8, 8, 16, 128), BF16),
            pltpu.VMEM((4, 2, 4, 16, 512), BF16),
            pltpu.VMEM((4, 2, 4, 16, 512), BF16),
            pltpu.VMEM((2, 8, 8, 16, 128), BF16),
            pltpu.VMEM((2, 64, 16, 128), BF16),
            pltpu.VMEM((8, 8, 2, 16, 128), BF16),
            pltpu.VMEM((64, 2, 16, 128), BF16),
            dma((3,)),
            dma((3,)),
            dma((3,)),
            dma((2, 2)),
            dma((4,)),
            dma((2,)),
            dma((2,)),
            dma((4,)),
            dma((4,)),
            dma((3,)),
            dma((3,)),
            dma((3,)),
            dma,
        ],
        compiler_params=pltpu.CompilerParams(
            collective_id=0, has_side_effects=True, vmem_limit_bytes=56 * 2**20
        ),
    )(pair_state, proj_weight, out_weight)
    return jnp.transpose(out, (1, 0, 2))


def solution(mesh):
    in_specs = (P("row", "col", None), P(), P())
    out_specs = P("row", "col", None)
    return jax.shard_map(shards, mesh=mesh, in_specs=in_specs, out_specs=out_specs, check_vma=False)
```

```python
import functools

import jax
import jax.numpy as jnp
from jax import lax
from jax.experimental import pallas as pl
from jax.experimental.pallas import tpu as pltpu
from jax.sharding import PartitionSpec as P

F32 = jnp.float32
BF16 = jnp.bfloat16
MESH = pl.DeviceIdType.MESH


def sigmoid(x):
    return 0.5 * jnp.tanh(0.5 * x) + 0.5


def normalize(x):
    center = x - jnp.mean(x, axis=0, keepdims=True)
    spread = jnp.mean(center * center, axis=0, keepdims=True)
    return center * lax.rsqrt(spread + 1e-05)


def interleave(even, odd):
    first = jnp.concatenate([even[..., :64], odd[..., :64]], axis=-1)
    second = jnp.concatenate([even[..., 64:], odd[..., 64:]], axis=-1)
    return first, second


def swap_blocks(x, axis):
    blocks = jnp.split(x, 4, axis=axis)
    return jnp.concatenate([blocks[0], blocks[2], blocks[1], blocks[3]], axis=axis)


def kernel(
    pair_hbm,
    proj_hbm,
    out_proj_hbm,
    out_ref,
    pair_ref,
    proj_ref,
    out_proj_ref,
    proj_t,
    out_proj_t,
    state,
    normed,
    gating,
    staged,
    mixnorm,
    final,
    left_op0,
    left_op1,
    partial,
    send_left,
    send_left1,
    send_right0,
    send_right,
    recv_left,
    recv_left1,
    recv_right0,
    recv_right,
    right_op,
    sibling_left,
    half_send,
    half_recv,
    send_half,
    recv_half,
    send_whole,
    recv_whole,
    left_send_sem,
    left_recv_sem,
    right_send_sem,
    right_recv0_sem,
    right_recv_sem,
    sib_send_sem,
    sib_recv_sem,
    half_send_sem,
    half_recv_sem,
    mixed_send_sem,
    mixed_recv_sem,
    load_sem,
    out_sem,
):
    r = lax.axis_index("row")
    col = lax.axis_index("col")
    q = col // 2
    core = col % 2
    chip = r * 8 + q

    def around(place):
        return [lax.rem(place // 4 + d // 4, 2) * 4 + lax.rem(place % 4 + d % 4, 4) for d in range(8)]

    rs, qs = around(r), around(q)

    def group_of(place):
        return place // 4 * 2 + place % 2

    def place_of(group, one):
        return group // 2 * 4 + group % 2 + 2 * one

    start = lax.rem(r % 4 + q // 4 * 2 + q % 4, 4)
    turns = [lax.rem(start + t, 4) for t in range(4)]

    sets = [lax.rem(r + q + t, 2) for t in range(2)]
    cols = [dest_q * 2 + core for dest_q in qs]
    sibling = (r, q * 2 + 1 - core)
    def hops(d, turn):
        return d // 4 * turn + min(d % 4, 4 - d % 4)

    far_r = sorted(range(8), key=lambda d: -hops(d, 2))
    far_q = sorted(range(8), key=lambda d: -hops(d, 1))
    others = [(d // 8, d % 8) for d in sorted(range(1, 64), key=lambda e: (e * 7919) % 1009)]
    others.sort(key=lambda d: -hops(d[0], 2) - hops(d[1], 1))

    loads = [
        pltpu.make_async_copy(src, dst, load_sem.at[i])
        for i, (src, dst) in enumerate(
            ((pair_hbm, pair_ref), (proj_hbm, proj_ref), (out_proj_hbm, out_proj_ref))
        )
    ]
    for load in loads:
        load.start()

    barrier = pltpu.get_barrier_semaphore()

    for dr, dq in others:
        pl.semaphore_signal(barrier, inc=1, device_id=(rs[dr], cols[dq]), device_id_type=MESH)
    pl.semaphore_signal(barrier, inc=1, device_id=sibling, device_id_type=MESH)

    loads[0].wait()
    pair = jnp.swapaxes(swap_blocks(pair_ref[...], 0), 0, 1)
    for half in range(2):
        for part in range(2):
            first = 16 * half + 8 * part
            final[part, 8 * half : 8 * half + 8] = pair[first : first + 8]

    def enter(t, carry):
        for h in range(2):
            block = final[:, 2 * t + h].reshape(128, 128).astype(F32).T
            state[t, :, 128 * h : 128 * h + 128] = block
        normed[t] = normalize(state[t]).astype(BF16)
        return carry

    lax.fori_loop(0, 8, enter, 0, unroll=8)
    for load in loads[1:]:
        load.wait()
    for u in range(2):
        proj_t[u] = proj_ref[u].T
        out_proj_t[u] = out_proj_ref[u].T

    def gated(u, first, tiles):
        for t in tiles:
            p = jnp.dot(proj_t[u, first : first + 256], normed[t], preferred_element_type=F32)
            value = sigmoid(p[:128]) * p[128:]
            for h in range(2):
                staged[2 * t + h] = value[:, 128 * h : 128 * h + 128].astype(BF16)
        return jnp.swapaxes(staged[2 * tiles[0] : 2 * tiles[-1] + 2], 0, 1)

    def whole_left(u):
        send_left[...] = gated(u, 0, range(8)).reshape(8, 8, 2, 16, 128)

    def half_left(half):
        value = gated(1, 0, range(4 * half, 4 * half + 4)).astype(F32)
        send_left1[half] = value.reshape(8, 8, 16, 128).astype(BF16)

    def half_rights():
        value = gated(0, 256, range(8)).astype(F32)
        low, high = value[:, :8], value[:, 8:]
        for half in range(2):
            lanes = [slice(32 * half + 64 * part, 32 * half + 64 * part + 32) for part in range(2)]
            pieces = jnp.concatenate([tile[..., at] for tile in (low, high) for at in lanes], axis=-1)
            send_right0[half] = pieces.reshape(8, 8, 16, 128).astype(BF16)

    def whole_right():
        send_right[...] = gated(1, 256, range(8)).reshape(8, 8, 2, 16, 128)

    def gate(u):
        def step(t, carry):
            p = jnp.dot(proj_t[u, 512:640], normed[t], preferred_element_type=F32)
            gating[t] = sigmoid(p)
            return carry

        lax.fori_loop(0, 8, step, 0, unroll=8)

    def push(src, dst, send_sem, recv_sem, device):
        pltpu.make_async_remote_copy(
            src_ref=src,
            dst_ref=dst,
            send_sem=send_sem,
            recv_sem=recv_sem,
            device_id=device,
            device_id_type=MESH,
        ).start()

    def push_or_keep(here, src, dst, send_sem, recv_sem, device):
        @pl.when(here)
        def _():
            pltpu.make_async_copy(src, dst, recv_sem).start()

        @pl.when(jnp.logical_not(here))
        def _():
            push(src, dst, send_sem, recv_sem, device)

    def send_all_left(src, slot, send_sem, recv_sem):
        pltpu.make_async_copy(src.at[r, q], slot, recv_sem).start()
        for dr, dq in others:
            push(src.at[rs[dr], qs[dq]], slot, send_sem, recv_sem, (rs[dr], cols[dq]))

    def send_whole_left():
        send_all_left(send_left, recv_left.at[r, q], left_send_sem.at[2], left_recv_sem.at[2])

    def send_half_left(half):
        send_all_left(
            send_left1.at[half], recv_left1.at[half, q, r], left_send_sem.at[half], left_recv_sem.at[half]
        )

    def send_half_right(half):
        mine = r % 2
        slot = recv_right0.at[half, mine, r // 2, q]
        send_sem, recv_sem = right_send_sem.at[half], right_recv0_sem.at[half, mine]
        for t in range(2):
            for a, d in [(a, d) for d in far_q for a in (2, 3, 1, 0)]:
                dest_q = qs[d]
                dest_r = lax.rem(r // 2 + a, 4) * 2 + lax.rem(mine + t + dest_q, 2)
                col = cols[d]
                src = send_right0.at[half, dest_r, dest_q]
                if a or d:
                    push(src, slot, send_sem, recv_sem, (dest_r, col))
                else:
                    push_or_keep(dest_r == r, src, slot, send_sem, recv_sem, (dest_r, col))

    def send_whole_right():
        mine = group_of(q)
        slot = recv_right.at[mine, q % 4 // 2, r]
        send_sem, recv_sem = right_send_sem.at[2], right_recv_sem.at[mine]
        for t in range(4):
            for dz in (1, 0):
                dest_rz = rs[4 * dz] // 4 * 4
                for d in far_q:
                    dest_q = qs[d]
                    dest_r = dest_rz + lax.rem(mine + 16 - t - dest_q // 4 * 2 - dest_q % 4, 4)
                    src = send_right.at[dest_r, dest_q]
                    if dz or d:
                        push(src, slot, send_sem, recv_sem, (dest_r, cols[d]))
                    else:
                        push_or_keep(dest_r == r, src, slot, send_sem, recv_sem, (dest_r, cols[d]))

    def give_half(half, members, values):
        for one, dest_q in enumerate(members):
            low, high = (
                jnp.concatenate([v[one, at : at + 8] for v in values], axis=0).astype(BF16) for at in (0, 8)
            )
            for m in range(4):
                lanes = slice(128 * m, 128 * m + 128)
                first, second = interleave(low[:, lanes], high[:, lanes])
                send_half[half, dest_q, 2 * m] = first
                send_half[half, dest_q, 2 * m + 1] = second

    def give_whole(group, c, value):
        for one in range(2):
            for m in range(4):
                lanes = slice(128 * m, 128 * m + 128)
                first, second = interleave(value[one, :16, lanes], value[one, 16:, lanes])
                send_whole[place_of(group, one), 2 * m, c] = first
                send_whole[place_of(group, one), 2 * m + 1, c] = second

    def send_back(src, slot, send_sem, recv_sem, members):
        for d in far_r:
            for dest_q in members:
                dest = (rs[d], dest_q * 2 + core)
                if d:
                    push(src.at[dest_q, rs[d]], slot, send_sem, recv_sem, dest)
                else:
                    push_or_keep(dest_q == q, src.at[dest_q, r], slot, send_sem, recv_sem, dest)

    def send_half_back(half, members):
        send_back(
            send_half.at[half], recv_half.at[half, chip], mixed_send_sem.at[half], mixed_recv_sem.at[half], members
        )

    def send_whole_back(group):
        members = [place_of(group, one) for one in range(2)]
        send_back(send_whole, recv_whole.at[chip], mixed_send_sem.at[2], mixed_recv_sem.at[2], members)

    def wait_all(ref, sem):
        pltpu.make_async_copy(ref, ref, sem).wait()

    def outgoing():
        wait_all(recv_left, left_recv_sem.at[2])
        for c in range(2):
            for m in range(4):
                first, second = interleave(recv_left[2 * m, :, c], recv_left[2 * m + 1, :, c])
                left_op0[c, 0, :, :, 128 * m : 128 * m + 128] = first
                left_op0[c, 1, :, :, 128 * m : 128 * m + 128] = second

        def half_copy(t):
            return pltpu.make_async_remote_copy(
                src_ref=half_send.at[t],
                dst_ref=half_recv.at[t],
                send_sem=half_send_sem.at[t],
                recv_sem=half_recv_sem.at[t],
                device_id=sibling,
                device_id_type=MESH,
            )

        def members_of(t):
            return [2 * one + sets[t % 2] for one in range(4)]

        def finish(t):
            half_copy(t).wait_recv()
            totals = [partial[t % 2, c, :, core] + half_recv[t, c].astype(F32) for c in range(2)]
            give_half(t // 2, members_of(t), totals)
            send_half_back(t // 2, members_of(t))

        for t in range(4):
            half, which = t // 2, sets[t % 2]
            wait_all(recv_right0.at[half, which], right_recv0_sem.at[half, which])
            for piece in range(4):
                lanes = slice(32 * piece, 32 * piece + 32)
                block = jnp.concatenate([recv_right0[half, which, one, :, :, lanes] for one in range(4)], axis=-1)
                high, part = piece // 2, piece % 2
                for c in range(2):
                    right_op[c, part, :, 8 * high : 8 * high + 8] = block[:, 8 * c : 8 * c + 8]
            for c in range(2):
                product = lax.dot_general(
                    right_op[c].reshape(256, 128),
                    left_op0[c].reshape(256, 512),
                    (((0,), (0,)), ((), ())),
                    preferred_element_type=F32,
                )
                partial[t % 2, c] = product.reshape(4, 2, 16, 512)
                half_send[t, c] = partial[t % 2, c, :, 1 - core].astype(BF16)
            half_copy(t).start()
            if t:
                finish(t - 1)
        finish(3)
        for t in range(4):
            half_copy(t).wait_send()

    def incoming():
        def arrange(ref, half, which):
            for m in range(4):
                pieces = interleave(ref[half, :, 2 * m], ref[half, :, 2 * m + 1])
                for part in range(2):
                    for c in range(2):
                        left_op1[c, :, half, which, 8 * part : 8 * part + 8, 128 * m : 128 * m + 128] = pieces[
                            part
                        ][:, 8 * c : 8 * c + 8]

        swaps = []
        for half in range(2):
            wait_all(recv_left1.at[half], left_recv_sem.at[half])
            swap = pltpu.make_async_remote_copy(
                src_ref=recv_left1.at[half],
                dst_ref=sibling_left.at[half],
                send_sem=sib_send_sem.at[half],
                recv_sem=sib_recv_sem.at[half],
                device_id=sibling,
                device_id_type=MESH,
            )
            swap.start()
            swaps.append(swap)
            arrange(recv_left1, half, core)
        for half in range(2):
            swaps[half].wait_recv()
            arrange(sibling_left, half, 1 - core)

        for t in range(4):
            group = turns[t]
            wait_all(recv_right.at[group], right_recv_sem.at[group])
            for c in range(2):
                columns = []
                for m in range(4):
                    even = recv_right[group, :, 2 * m, c]
                    odd = recv_right[group, :, 2 * m + 1, c]
                    columns.append(jnp.stack(interleave(even, odd), axis=1).reshape(64, 128))
                right = jnp.concatenate(columns, axis=1)
                product = lax.dot_general(
                    right, left_op1[c].reshape(512, 512), (((1,), (1,)), ((), ())), preferred_element_type=F32
                )
                give_whole(group, c, product.astype(BF16).reshape(2, 32, 512))
            send_whole_back(group)
        for swap in swaps:
            swap.wait_send()

    def absorb_half(half):
        wait_all(recv_half.at[half], mixed_recv_sem.at[half])
        norm = normalize(recv_half[half].astype(F32).reshape(128, 8, 128))
        norm = jnp.swapaxes(norm, 0, 1).astype(BF16)
        for t in range(4 * half, 4 * half + 4):
            for h in range(2):
                mixnorm[t, :, 128 * h : 128 * h + 128] = norm[2 * t + h - 8 * half]
            output = jnp.dot(out_proj_t[0], mixnorm[t], preferred_element_type=F32)
            updated = (state[t] + gating[t] * output).astype(BF16).astype(F32)
            state[t] = updated
            normed[t] = normalize(updated).astype(BF16)

    def absorb_whole():
        wait_all(recv_whole, mixed_recv_sem.at[2])
        norm = normalize(recv_whole[...].reshape(128, 16, 128).astype(F32))
        norm = jnp.swapaxes(norm.astype(BF16), 0, 1)
        for t in range(8):
            for h in range(2):
                mixnorm[t, :, 128 * h : 128 * h + 128] = norm[2 * t + h]
            output = jnp.dot(out_proj_t[1], mixnorm[t], preferred_element_type=F32)
            updated = state[t] + gating[t] * output
            for h in range(2):
                block = updated[:, 128 * h : 128 * h + 128].T.astype(BF16)
                final[:, 2 * t + h] = swap_blocks(block.reshape(2, 64, 128), 1)
            for part in range(2):
                column = 16 * (t // 4) + 8 * part + 2 * t % 8
                pltpu.make_async_copy(
                    final.at[part, pl.ds(2 * t, 2)], out_ref.at[pl.ds(column, 2)], out_sem
                ).start()

    whole_left(0)
    pl.semaphore_wait(barrier, 64)
    send_whole_left()
    half_rights()
    for half in range(2):
        send_half_right(half)
    gate(0)
    outgoing()
    for half in range(2):
        absorb_half(half)
        half_left(half)
        send_half_left(half)
    whole_right()
    send_whole_right()
    gate(1)
    incoming()
    absorb_whole()

    for half in range(2):
        wait_all(recv_half.at[half, pl.ds(0, 63)], left_send_sem.at[half])
        wait_all(recv_half.at[half, pl.ds(0, 63)], right_send_sem.at[half])
        wait_all(recv_half.at[half, pl.ds(0, 63)], mixed_send_sem.at[half])
    for sem in (left_send_sem.at[2], right_send_sem.at[2], mixed_send_sem.at[2]):
        wait_all(recv_whole.at[pl.ds(0, 63)], sem)
    wait_all(out_ref, out_sem)


def shards(pair_state, proj_weight, out_weight):
    dma = pltpu.SemaphoreType.DMA
    out = pl.pallas_call(
        kernel,
        out_shape=jax.ShapeDtypeStruct((32, 64, 128), BF16),
        in_specs=[pl.BlockSpec(memory_space=pl.ANY)] * 3,
        out_specs=pl.BlockSpec(memory_space=pl.ANY),
        scratch_shapes=[
            pltpu.VMEM((64, 32, 128), BF16),
            pltpu.VMEM((2, 128, 640), BF16),
            pltpu.VMEM((2, 128, 128), BF16),
            pltpu.VMEM((2, 640, 128), BF16),
            pltpu.VMEM((2, 128, 128), BF16),
            pltpu.VMEM((8, 128, 256), F32),
            pltpu.VMEM((8, 128, 256), BF16),
            pltpu.VMEM((8, 128, 256), F32),
            pltpu.VMEM((16, 128, 128), BF16),
            pltpu.VMEM((8, 128, 256), BF16),
            pltpu.VMEM((2, 16, 64, 128), BF16),
            pltpu.VMEM((2, 2, 8, 16, 512), BF16),
            pltpu.VMEM((2, 8, 2, 2, 16, 512), BF16),
            pltpu.VMEM((2, 2, 4, 2, 16, 512), F32),
            pltpu.VMEM((8, 8, 2, 16, 128), BF16),
            pltpu.VMEM((2, 8, 8, 16, 128), BF16),
            pltpu.VMEM((2, 8, 8, 16, 128), BF16),
            pltpu.VMEM((8, 8, 2, 16, 128), BF16),
            pltpu.VMEM((8, 8, 2, 16, 128), BF16),
            pltpu.VMEM((2, 8, 8, 16, 128), BF16),
            pltpu.VMEM((2, 2, 4, 8, 16, 128), BF16),
            pltpu.VMEM((4, 2, 8, 2, 16, 128), BF16),
            pltpu.VMEM((2, 2, 8, 16, 128), BF16),
            pltpu.VMEM((2, 8, 8, 16, 128), BF16),
            pltpu.VMEM((4, 2, 4, 16, 512), BF16),
            pltpu.VMEM((4, 2, 4, 16, 512), BF16),
            pltpu.VMEM((2, 8, 8, 16, 128), BF16),
            pltpu.VMEM((2, 64, 16, 128), BF16),
            pltpu.VMEM((8, 8, 2, 16, 128), BF16),
            pltpu.VMEM((64, 2, 16, 128), BF16),
            dma((3,)),
            dma((3,)),
            dma((3,)),
            dma((2, 2)),
            dma((4,)),
            dma((2,)),
            dma((2,)),
            dma((4,)),
            dma((4,)),
            dma((3,)),
            dma((3,)),
            dma((3,)),
            dma,
        ],
        compiler_params=pltpu.CompilerParams(
            collective_id=0, has_side_effects=True, vmem_limit_bytes=56 * 2**20
        ),
    )(pair_state, proj_weight, out_weight)
    return jnp.transpose(out, (1, 0, 2))


def solution(mesh):
    in_specs = (P("row", "col", None), P(), P())
    out_specs = P("row", "col", None)
    return jax.shard_map(shards, mesh=mesh, in_specs=in_specs, out_specs=out_specs, check_vma=False)
```

```python
import functools

import jax
import jax.numpy as jnp
from jax import lax
from jax.experimental import pallas as pl
from jax.experimental.pallas import tpu as pltpu
from jax.sharding import PartitionSpec as P

F32 = jnp.float32
BF16 = jnp.bfloat16
MESH = pl.DeviceIdType.MESH


def sigmoid(x):
    return 0.5 * jnp.tanh(0.5 * x) + 0.5


def normalize(x):
    center = x - jnp.mean(x, axis=0, keepdims=True)
    spread = jnp.mean(center * center, axis=0, keepdims=True)
    return center * lax.rsqrt(spread + 1e-05)


def interleave(even, odd):
    first = jnp.concatenate([even[..., :64], odd[..., :64]], axis=-1)
    second = jnp.concatenate([even[..., 64:], odd[..., 64:]], axis=-1)
    return first, second


def swap_blocks(x, axis):
    blocks = jnp.split(x, 4, axis=axis)
    return jnp.concatenate([blocks[0], blocks[2], blocks[1], blocks[3]], axis=axis)


def kernel(
    pair_hbm,
    proj_hbm,
    out_proj_hbm,
    out_ref,
    pair_ref,
    proj_ref,
    out_proj_ref,
    proj_t,
    out_proj_t,
    state,
    normed,
    gating,
    staged,
    mixnorm,
    final,
    left_op0,
    left_op1,
    partial,
    send_left,
    send_left1,
    send_right0,
    send_right,
    recv_left,
    recv_left1,
    recv_right0,
    recv_right,
    right_op,
    sibling_left,
    half_send,
    half_recv,
    send_half,
    recv_half,
    send_whole,
    recv_whole,
    left_send_sem,
    left_recv_sem,
    right_send_sem,
    right_recv0_sem,
    right_recv_sem,
    sib_send_sem,
    sib_recv_sem,
    half_send_sem,
    half_recv_sem,
    mixed_send_sem,
    mixed_recv_sem,
    load_sem,
    out_sem,
):
    r = lax.axis_index("row")
    col = lax.axis_index("col")
    q = col // 2
    core = col % 2
    chip = r * 8 + q

    def around(place):
        return [lax.rem(place // 4 + d // 4, 2) * 4 + lax.rem(place % 4 + d % 4, 4) for d in range(8)]

    rs, qs = around(r), around(q)

    def group_of(place):
        return place // 4 * 2 + place % 2

    def place_of(group, one):
        return group // 2 * 4 + group % 2 + 2 * one

    start = lax.rem(r % 4 + q // 4 * 2 + q % 4, 4)
    turns = [lax.rem(start + t, 4) for t in range(4)]

    sets = [lax.rem(r + q + t, 2) for t in range(2)]
    cols = [dest_q * 2 + core for dest_q in qs]
    sibling = (r, q * 2 + 1 - core)
    def hops(d, turn):
        return d // 4 * turn + min(d % 4, 4 - d % 4)

    far_r = sorted(range(8), key=lambda d: -hops(d, 2))
    far_q = sorted(range(8), key=lambda d: -hops(d, 1))
    others = [(d // 8, d % 8) for d in sorted(range(1, 64), key=lambda e: (e * 7919) % 1009)]
    others.sort(key=lambda d: -hops(d[0], 2) - hops(d[1], 1))

    loads = [
        pltpu.make_async_copy(src, dst, load_sem.at[i])
        for i, (src, dst) in enumerate(
            ((pair_hbm, pair_ref), (proj_hbm, proj_ref), (out_proj_hbm, out_proj_ref))
        )
    ]
    for load in loads:
        load.start()

    barrier = pltpu.get_barrier_semaphore()

    for dr, dq in others:
        pl.semaphore_signal(barrier, inc=1, device_id=(rs[dr], cols[dq]), device_id_type=MESH)
    pl.semaphore_signal(barrier, inc=1, device_id=sibling, device_id_type=MESH)

    loads[0].wait()
    pair = jnp.swapaxes(swap_blocks(pair_ref[...], 0), 0, 1)
    for half in range(2):
        for part in range(2):
            first = 16 * half + 8 * part
            final[part, 8 * half : 8 * half + 8] = pair[first : first + 8]

    def enter(t, carry):
        for h in range(2):
            block = final[:, 2 * t + h].reshape(128, 128).astype(F32).T
            state[t, :, 128 * h : 128 * h + 128] = block
        normed[t] = normalize(state[t]).astype(BF16)
        return carry

    lax.fori_loop(0, 8, enter, 0, unroll=8)
    for load in loads[1:]:
        load.wait()
    for u in range(2):
        proj_t[u] = proj_ref[u].T
        out_proj_t[u] = out_proj_ref[u].T

    def gated(u, first, tiles):
        for t in tiles:
            p = jnp.dot(proj_t[u, first : first + 256], normed[t], preferred_element_type=F32)
            value = sigmoid(p[:128]) * p[128:]
            for h in range(2):
                staged[2 * t + h] = value[:, 128 * h : 128 * h + 128].astype(BF16)
        return jnp.swapaxes(staged[2 * tiles[0] : 2 * tiles[-1] + 2], 0, 1)

    def whole_left(u):
        send_left[...] = gated(u, 0, range(8)).reshape(8, 8, 2, 16, 128)

    def half_left(half):
        value = gated(1, 0, range(4 * half, 4 * half + 4)).astype(F32)
        send_left1[half] = value.reshape(8, 8, 16, 128).astype(BF16)

    def half_rights():
        value = gated(0, 256, range(8)).astype(F32)
        low, high = value[:, :8], value[:, 8:]
        for half in range(2):
            lanes = [slice(32 * half + 64 * part, 32 * half + 64 * part + 32) for part in range(2)]
            pieces = jnp.concatenate([tile[..., at] for tile in (low, high) for at in lanes], axis=-1)
            send_right0[half] = pieces.reshape(8, 8, 16, 128).astype(BF16)

    def whole_right():
        send_right[...] = gated(1, 256, range(8)).reshape(8, 8, 2, 16, 128)

    def gate(u):
        def step(t, carry):
            p = jnp.dot(proj_t[u, 512:640], normed[t], preferred_element_type=F32)
            gating[t] = sigmoid(p)
            return carry

        lax.fori_loop(0, 8, step, 0, unroll=8)

    def push(src, dst, send_sem, recv_sem, device):
        pltpu.make_async_remote_copy(
            src_ref=src,
            dst_ref=dst,
            send_sem=send_sem,
            recv_sem=recv_sem,
            device_id=device,
            device_id_type=MESH,
        ).start()

    def push_or_keep(here, src, dst, send_sem, recv_sem, device):
        @pl.when(here)
        def _():
            pltpu.make_async_copy(src, dst, recv_sem).start()

        @pl.when(jnp.logical_not(here))
        def _():
            push(src, dst, send_sem, recv_sem, device)

    def send_all_left(src, slot, send_sem, recv_sem):
        pltpu.make_async_copy(src.at[r, q], slot, recv_sem).start()
        for dr, dq in others:
            push(src.at[rs[dr], qs[dq]], slot, send_sem, recv_sem, (rs[dr], cols[dq]))

    def send_whole_left():
        send_all_left(send_left, recv_left.at[r, q], left_send_sem.at[2], left_recv_sem.at[2])

    def send_half_left(half):
        send_all_left(
            send_left1.at[half], recv_left1.at[half, q, r], left_send_sem.at[half], left_recv_sem.at[half]
        )

    def send_half_right(half):
        mine = r % 2
        slot = recv_right0.at[half, mine, r // 2, q]
        send_sem, recv_sem = right_send_sem.at[half], right_recv0_sem.at[half, mine]
        for t in range(2):
            for a, d in [(a, d) for d in far_q for a in (2, 3, 1, 0)]:
                dest_q = qs[d]
                dest_r = lax.rem(r // 2 + a, 4) * 2 + lax.rem(mine + t + dest_q, 2)
                col = cols[d]
                src = send_right0.at[half, dest_r, dest_q]
                if a or d:
                    push(src, slot, send_sem, recv_sem, (dest_r, col))
                else:
                    push_or_keep(dest_r == r, src, slot, send_sem, recv_sem, (dest_r, col))

    def send_whole_right():
        mine = group_of(q)
        slot = recv_right.at[mine, q % 4 // 2, r]
        send_sem, recv_sem = right_send_sem.at[2], right_recv_sem.at[mine]
        for t in range(4):
            for dz in (1, 0):
                dest_rz = rs[4 * dz] // 4 * 4
                for d in far_q:
                    dest_q = qs[d]
                    dest_r = dest_rz + lax.rem(mine + 16 - t - dest_q // 4 * 2 - dest_q % 4, 4)
                    src = send_right.at[dest_r, dest_q]
                    if dz or d:
                        push(src, slot, send_sem, recv_sem, (dest_r, cols[d]))
                    else:
                        push_or_keep(dest_r == r, src, slot, send_sem, recv_sem, (dest_r, cols[d]))

    def give_half(half, members, values):
        for one, dest_q in enumerate(members):
            low, high = (
                jnp.concatenate([v[one, at : at + 8] for v in values], axis=0).astype(BF16) for at in (0, 8)
            )
            for m in range(4):
                lanes = slice(128 * m, 128 * m + 128)
                first, second = interleave(low[:, lanes], high[:, lanes])
                send_half[half, dest_q, 2 * m] = first
                send_half[half, dest_q, 2 * m + 1] = second

    def give_whole(group, c, value):
        for one in range(2):
            for m in range(4):
                lanes = slice(128 * m, 128 * m + 128)
                first, second = interleave(value[one, :16, lanes], value[one, 16:, lanes])
                send_whole[place_of(group, one), 2 * m, c] = first
                send_whole[place_of(group, one), 2 * m + 1, c] = second

    def send_back(src, slot, send_sem, recv_sem, members):
        for d in far_r:
            for dest_q in members:
                dest = (rs[d], dest_q * 2 + core)
                if d:
                    push(src.at[dest_q, rs[d]], slot, send_sem, recv_sem, dest)
                else:
                    push_or_keep(dest_q == q, src.at[dest_q, r], slot, send_sem, recv_sem, dest)

    def send_half_back(half, members):
        send_back(
            send_half.at[half], recv_half.at[half, chip], mixed_send_sem.at[half], mixed_recv_sem.at[half], members
        )

    def send_whole_back(group):
        members = [place_of(group, one) for one in range(2)]
        send_back(send_whole, recv_whole.at[chip], mixed_send_sem.at[2], mixed_recv_sem.at[2], members)

    def wait_all(ref, sem):
        pltpu.make_async_copy(ref, ref, sem).wait()

    def outgoing():
        wait_all(recv_left, left_recv_sem.at[2])
        for c in range(2):
            for m in range(4):
                first, second = interleave(recv_left[2 * m, :, c], recv_left[2 * m + 1, :, c])
                left_op0[c, 0, :, :, 128 * m : 128 * m + 128] = first
                left_op0[c, 1, :, :, 128 * m : 128 * m + 128] = second

        def half_copy(t):
            return pltpu.make_async_remote_copy(
                src_ref=half_send.at[t],
                dst_ref=half_recv.at[t],
                send_sem=half_send_sem.at[t],
                recv_sem=half_recv_sem.at[t],
                device_id=sibling,
                device_id_type=MESH,
            )

        def members_of(t):
            return [2 * one + sets[t % 2] for one in range(4)]

        def finish(t):
            half_copy(t).wait_recv()
            totals = [partial[t % 2, c, :, core] + half_recv[t, c].astype(F32) for c in range(2)]
            give_half(t // 2, members_of(t), totals)
            if t != 2:
                send_half_back(t // 2, members_of(t) if t < 2 else members_of(2) + members_of(3))

        for t in range(4):
            half, which = t // 2, sets[t % 2]
            wait_all(recv_right0.at[half, which], right_recv0_sem.at[half, which])
            for piece in range(4):
                lanes = slice(32 * piece, 32 * piece + 32)
                block = jnp.concatenate([recv_right0[half, which, one, :, :, lanes] for one in range(4)], axis=-1)
                high, part = piece // 2, piece % 2
                for c in range(2):
                    right_op[c, part, :, 8 * high : 8 * high + 8] = block[:, 8 * c : 8 * c + 8]
            for c in range(2):
                product = lax.dot_general(
                    right_op[c].reshape(256, 128),
                    left_op0[c].reshape(256, 512),
                    (((0,), (0,)), ((), ())),
                    preferred_element_type=F32,
                )
                partial[t % 2, c] = product.reshape(4, 2, 16, 512)
                half_send[t, c] = partial[t % 2, c, :, 1 - core].astype(BF16)
            half_copy(t).start()
            if t:
                finish(t - 1)
        finish(3)
        for t in range(4):
            half_copy(t).wait_send()

    def incoming():
        def arrange(ref, half, which):
            for m in range(4):
                pieces = interleave(ref[half, :, 2 * m], ref[half, :, 2 * m + 1])
                for part in range(2):
                    for c in range(2):
                        left_op1[c, :, half, which, 8 * part : 8 * part + 8, 128 * m : 128 * m + 128] = pieces[
                            part
                        ][:, 8 * c : 8 * c + 8]

        swaps = []
        for half in range(2):
            wait_all(recv_left1.at[half], left_recv_sem.at[half])
            swap = pltpu.make_async_remote_copy(
                src_ref=recv_left1.at[half],
                dst_ref=sibling_left.at[half],
                send_sem=sib_send_sem.at[half],
                recv_sem=sib_recv_sem.at[half],
                device_id=sibling,
                device_id_type=MESH,
            )
            swap.start()
            swaps.append(swap)
            arrange(recv_left1, half, core)
        for half in range(2):
            swaps[half].wait_recv()
            arrange(sibling_left, half, 1 - core)

        for t in range(4):
            group = turns[t]
            wait_all(recv_right.at[group], right_recv_sem.at[group])
            for c in range(2):
                columns = []
                for m in range(4):
                    even = recv_right[group, :, 2 * m, c]
                    odd = recv_right[group, :, 2 * m + 1, c]
                    columns.append(jnp.stack(interleave(even, odd), axis=1).reshape(64, 128))
                right = jnp.concatenate(columns, axis=1)
                product = lax.dot_general(
                    right, left_op1[c].reshape(512, 512), (((1,), (1,)), ((), ())), preferred_element_type=F32
                )
                give_whole(group, c, product.astype(BF16).reshape(2, 32, 512))
            send_whole_back(group)
        for swap in swaps:
            swap.wait_send()

    def absorb_half(half):
        wait_all(recv_half.at[half], mixed_recv_sem.at[half])
        norm = normalize(recv_half[half].astype(F32).reshape(128, 8, 128))
        norm = jnp.swapaxes(norm, 0, 1).astype(BF16)
        for t in range(4 * half, 4 * half + 4):
            for h in range(2):
                mixnorm[t, :, 128 * h : 128 * h + 128] = norm[2 * t + h - 8 * half]
            output = jnp.dot(out_proj_t[0], mixnorm[t], preferred_element_type=F32)
            updated = (state[t] + gating[t] * output).astype(BF16).astype(F32)
            state[t] = updated
            normed[t] = normalize(updated).astype(BF16)

    def absorb_whole():
        wait_all(recv_whole, mixed_recv_sem.at[2])
        norm = normalize(recv_whole[...].reshape(128, 16, 128).astype(F32))
        norm = jnp.swapaxes(norm.astype(BF16), 0, 1)
        for t in range(8):
            for h in range(2):
                mixnorm[t, :, 128 * h : 128 * h + 128] = norm[2 * t + h]
            output = jnp.dot(out_proj_t[1], mixnorm[t], preferred_element_type=F32)
            updated = state[t] + gating[t] * output
            for h in range(2):
                block = updated[:, 128 * h : 128 * h + 128].T.astype(BF16)
                final[:, 2 * t + h] = swap_blocks(block.reshape(2, 64, 128), 1)
            for part in range(2):
                column = 16 * (t // 4) + 8 * part + 2 * t % 8
                pltpu.make_async_copy(
                    final.at[part, pl.ds(2 * t, 2)], out_ref.at[pl.ds(column, 2)], out_sem
                ).start()

    whole_left(0)
    pl.semaphore_wait(barrier, 64)
    send_whole_left()
    half_rights()
    for half in range(2):
        send_half_right(half)
    gate(0)
    outgoing()
    for half in range(2):
        absorb_half(half)
        half_left(half)
        send_half_left(half)
    whole_right()
    send_whole_right()
    gate(1)
    incoming()
    absorb_whole()

    for half in range(2):
        wait_all(recv_half.at[half, pl.ds(0, 63)], left_send_sem.at[half])
        wait_all(recv_half.at[half, pl.ds(0, 63)], right_send_sem.at[half])
        wait_all(recv_half.at[half, pl.ds(0, 63)], mixed_send_sem.at[half])
    for sem in (left_send_sem.at[2], right_send_sem.at[2], mixed_send_sem.at[2]):
        wait_all(recv_whole.at[pl.ds(0, 63)], sem)
    wait_all(out_ref, out_sem)


def shards(pair_state, proj_weight, out_weight):
    dma = pltpu.SemaphoreType.DMA
    out = pl.pallas_call(
        kernel,
        out_shape=jax.ShapeDtypeStruct((32, 64, 128), BF16),
        in_specs=[pl.BlockSpec(memory_space=pl.ANY)] * 3,
        out_specs=pl.BlockSpec(memory_space=pl.ANY),
        scratch_shapes=[
            pltpu.VMEM((64, 32, 128), BF16),
            pltpu.VMEM((2, 128, 640), BF16),
            pltpu.VMEM((2, 128, 128), BF16),
            pltpu.VMEM((2, 640, 128), BF16),
            pltpu.VMEM((2, 128, 128), BF16),
            pltpu.VMEM((8, 128, 256), F32),
            pltpu.VMEM((8, 128, 256), BF16),
            pltpu.VMEM((8, 128, 256), F32),
            pltpu.VMEM((16, 128, 128), BF16),
            pltpu.VMEM((8, 128, 256), BF16),
            pltpu.VMEM((2, 16, 64, 128), BF16),
            pltpu.VMEM((2, 2, 8, 16, 512), BF16),
            pltpu.VMEM((2, 8, 2, 2, 16, 512), BF16),
            pltpu.VMEM((2, 2, 4, 2, 16, 512), F32),
            pltpu.VMEM((8, 8, 2, 16, 128), BF16),
            pltpu.VMEM((2, 8, 8, 16, 128), BF16),
            pltpu.VMEM((2, 8, 8, 16, 128), BF16),
            pltpu.VMEM((8, 8, 2, 16, 128), BF16),
            pltpu.VMEM((8, 8, 2, 16, 128), BF16),
            pltpu.VMEM((2, 8, 8, 16, 128), BF16),
            pltpu.VMEM((2, 2, 4, 8, 16, 128), BF16),
            pltpu.VMEM((4, 2, 8, 2, 16, 128), BF16),
            pltpu.VMEM((2, 2, 8, 16, 128), BF16),
            pltpu.VMEM((2, 8, 8, 16, 128), BF16),
            pltpu.VMEM((4, 2, 4, 16, 512), BF16),
            pltpu.VMEM((4, 2, 4, 16, 512), BF16),
            pltpu.VMEM((2, 8, 8, 16, 128), BF16),
            pltpu.VMEM((2, 64, 16, 128), BF16),
            pltpu.VMEM((8, 8, 2, 16, 128), BF16),
            pltpu.VMEM((64, 2, 16, 128), BF16),
            dma((3,)),
            dma((3,)),
            dma((3,)),
            dma((2, 2)),
            dma((4,)),
            dma((2,)),
            dma((2,)),
            dma((4,)),
            dma((4,)),
            dma((3,)),
            dma((3,)),
            dma((3,)),
            dma,
        ],
        compiler_params=pltpu.CompilerParams(
            collective_id=0, has_side_effects=True, vmem_limit_bytes=56 * 2**20
        ),
    )(pair_state, proj_weight, out_weight)
    return jnp.transpose(out, (1, 0, 2))


def solution(mesh):
    in_specs = (P("row", "col", None), P(), P())
    out_specs = P("row", "col", None)
    return jax.shard_map(shards, mesh=mesh, in_specs=in_specs, out_specs=out_specs, check_vma=False)
```
